256 devices in a mesh: region: 8 (over x, core), dev: 32 (over z, y).
Axes of the slice: x: 4, y: 4, z: 8, core: 2. Of those that a mesh axis runs over, the one named last changes fastest.
Arguments:
- synthetic: bfloat16 [4096, 3, 4096], P(('region', 'dev')), may hold values from -6 to 6
- observed: bfloat16 [4096, 3, 4096], P(('region', 'dev')), may hold values from -6 to 6
- nearby_receiver_slots: int32 [8192, 4], P(('region', 'dev')), may hold values from 0 to 15
- far_rows: int32 [8192, 4], P(('region', 'dev')), may hold values from 0 to 15
- first_slot: int32 [65536], P(('region', 'dev')), may hold values from 0 to 127
- second_slot: int32 [65536], P(('region', 'dev')), may hold values from 0 to 255
- window_start: int32 [65536], P(('region', 'dev')), may hold values from 0 to 255
- pair_delay_indices: int32 [65536], P(('region', 'dev')), may hold values from 64 to 256
Outputs:
- adjoint: bfloat16 [4096, 3, 4096], P(('region', 'dev'))
- misfit: float32 [65536], P(('region', 'dev'))
The draws below stay inside these ranges and needn't reach their ends.
All inputs are finite; a program needn't handle non-finite values.
Results may differ from the reference program's by a relative error of at most 0.0084.
Values may be sent and summed in bfloat16 or wider, within the bound.
No kernel may reach another device: no remote copies, remote signals or barrier semaphores. Data moves between devices by JAX's collectives and lax.ppermute only.
A program may use at most 128 MiB of HBM per device.

```python
import math
import jax
import jax.numpy as jnp
from jax import lax

NT = 4096
F = 512
FLOW = 64
LAGS = 512
RPD = 16
CAP = 4
PAIRS_DEV = 256
STATION_TOTAL = 4096
PAIRS = 65536
N_REGION = 8
N_DEV = 32
DEVICES = 256


def place_ends(entries, stream_key, least, top_value):
    longest = entries.shape.index(max(entries.shape))
    spots = []
    for shift in (0, 1):
        where = [jax.random.randint(jax.random.fold_in(stream_key, axis), (), 0, length) for axis, length in enumerate(entries.shape)]
        where[longest] = (where[longest] + shift) % entries.shape[longest]
        spots.append(tuple(where))
    return entries.at[spots[0]].set(least).at[spots[1]].set(top_value)


def level_of(key, extent, shards, smallest, top_value):
    loudness, own = 1.0, jax.random.fold_in(key, 6)
    for axis_at, parts in shards:
        steps = jnp.exp(jax.random.uniform(jax.random.fold_in(own, axis_at), (parts,), jnp.float32, smallest / len(shards), top_value / len(shards)))
        loudness = loudness * jnp.repeat(steps, extent[axis_at] // parts).reshape([-1 if axis == axis_at else 1 for axis in range(len(extent))])
    return loudness


def gaussian(own_key, extent, spread, most, split=(), kind=jnp.bfloat16):
    loudness = level_of(own_key, extent, split, -0.22, 0.18) if split else 1.0
    entries = jax.random.normal(own_key, extent, jnp.float32) * spread * loudness
    return jnp.minimum(jnp.maximum(entries, -most), most).astype(kind)


def setup_inputs(seed: int = 0) -> dict:
    seeds = jax.random.split(jax.random.key(seed), 9)
    synthetic = gaussian(seeds[0], (STATION_TOTAL, 3, NT), 1.0, 6.0, ((0, 256),))
    observed = gaussian(seeds[1], (STATION_TOTAL, 3, NT), 1.0, 6.0, ((0, 256),))
    nearby_receiver_slots = place_ends(jax.random.randint(seeds[2], (DEVICES * N_DEV, CAP), 0, RPD), jax.random.fold_in(seeds[2], 1), 0, RPD - 1).astype(jnp.int32)
    far_rows = place_ends(jax.random.randint(seeds[3], (DEVICES * N_DEV, CAP), 0, RPD), jax.random.fold_in(seeds[3], 1), 0, RPD - 1).astype(jnp.int32)
    first_slot = place_ends(jax.random.randint(seeds[4], (PAIRS,), 0, N_DEV * CAP), jax.random.fold_in(seeds[4], 1), 0, (N_DEV * CAP) - 1).astype(jnp.int32)
    second_slot = place_ends(jax.random.randint(seeds[5], (PAIRS,), 0, 2 * N_DEV * CAP), jax.random.fold_in(seeds[5], 1), 0, (2 * N_DEV * CAP) - 1).astype(jnp.int32)
    window_start = place_ends(jax.random.randint(seeds[6], (PAIRS,), 0, LAGS // 2), jax.random.fold_in(seeds[6], 1), 0, (LAGS // 2) - 1).astype(jnp.int32)
    pair_delay_indices = place_ends(jax.random.randint(seeds[7], (PAIRS,), LAGS // 8, LAGS // 2 + 1), jax.random.fold_in(seeds[7], 1), LAGS // 8, (LAGS // 2 + 1) - 1).astype(jnp.int32)
    return dict(synthetic=synthetic, observed=observed, nearby_receiver_slots=nearby_receiver_slots, far_rows=far_rows, first_slot=first_slot, second_slot=second_slot, window_start=window_start, pair_delay_indices=pair_delay_indices)


def make_tables(discrete_ticks):
    clock_moments = jnp.arange(discrete_ticks, dtype=jnp.int32)
    angular_rate = FLOW + jnp.arange(F, dtype=jnp.int32)
    oscillation_arguments = clock_moments[:, None] * angular_rate[None, :] % discrete_ticks
    angles = oscillation_arguments.astype(jnp.float32) * (2.0 * math.pi / discrete_ticks)
    forward = (jnp.concatenate([jnp.cos(angles), -jnp.sin(angles)], 1) / math.sqrt(discrete_ticks)).astype(jnp.bfloat16)
    shifts = jnp.arange(LAGS, dtype=jnp.int32) - LAGS // 2
    turning = angular_rate[:, None] * shifts[None, :] % discrete_ticks
    delay_rotation_matrix = turning.astype(jnp.float32) * (2.0 * math.pi / discrete_ticks)
    lag_lookup_table = (jnp.concatenate([jnp.cos(delay_rotation_matrix), -jnp.sin(delay_rotation_matrix)], 0) / math.sqrt(F)).astype(jnp.bfloat16)
    return (forward, lag_lookup_table)

def cross_power_spectrum(left, right):
    left_re, left_im = (left[..., :F], left[..., F:])
    right_re, right_im = (right[..., :F], right[..., F:])
    return jnp.concatenate([left_re * right_re + left_im * right_im, left_im * right_re - left_re * right_im], -1)

def pair_terms(first, second, starts, lengths, lag_lookup_table):
    first = first.astype(jnp.float32)
    second = second.astype(jnp.float32)
    change = (cross_power_spectrum(first[:, 0], second[:, 0]) - cross_power_spectrum(first[:, 1], second[:, 1])).astype(jnp.bfloat16)
    count = change.shape[0]
    shifted = jnp.dot(change.reshape(count * 3, 2 * F), lag_lookup_table, preferred_element_type=jnp.float32).reshape(count, 3, LAGS)
    position = jnp.arange(LAGS, dtype=jnp.int32)
    inside = (position[None, :] >= starts[:, None]) & (position[None, :] < (starts + lengths)[:, None])
    residual = jnp.where(inside[:, None, :], shifted, 0.0)
    misfit = lax.optimization_barrier(jnp.sum(residual * residual, axis=(1, 2))) / (2.0 * LAGS)
    slope = lax.dot_general(residual.astype(jnp.bfloat16).reshape(count * 3, LAGS), lag_lookup_table, (((1,), (1,)), ((), ())), preferred_element_type=jnp.float32).reshape(count, 3, 2 * F)
    slope_re, slope_im = (slope[..., :F], slope[..., F:])
    first_re, first_im = (first[:, 0, :, :F], first[:, 0, :, F:])
    second_re, second_im = (second[:, 0, :, :F], second[:, 0, :, F:])
    grad_first = jnp.concatenate([slope_re * second_re - slope_im * second_im, slope_re * second_im + slope_im * second_re], -1)
    grad_second = jnp.concatenate([slope_re * first_re + slope_im * first_im, slope_re * first_im - slope_im * first_re], -1)
    return (misfit, grad_first, grad_second)

def reference(synthetic, observed, nearby_receiver_slots, far_rows, first_slot, second_slot, window_start, pair_delay_indices):
    discrete_ticks = synthetic.shape[2]
    forward, lag_lookup_table = make_tables(discrete_ticks)

    def transform(traces):
        stacked = jnp.stack([traces[0], traces[1]], 1).reshape(RPD * 6, discrete_ticks)
        return jnp.dot(stacked, forward, preferred_element_type=jnp.float32).astype(jnp.bfloat16).reshape(RPD, 2, 3, 2 * F)
    spectra = lax.map(transform, (synthetic.reshape(DEVICES, RPD, 3, discrete_ticks), observed.reshape(DEVICES, RPD, 3, discrete_ticks)))
    spectra = spectra.reshape(N_REGION, N_DEV, RPD, 2, 3, 2 * F)
    padded = jnp.concatenate([spectra, jnp.zeros_like(spectra[:1])], 0)
    near_table = nearby_receiver_slots.reshape(N_REGION, N_DEV, N_DEV, CAP)
    far_table = far_rows.reshape(N_REGION, N_DEV, N_DEV, CAP)
    slot_count = 2 * N_DEV * CAP
    peer_index = jnp.arange(N_DEV, dtype=jnp.int32)[:, None]

    def visit(totals, owner):
        region = owner // N_DEV
        member = owner % N_DEV
        here = lax.dynamic_index_in_dim(padded, region, 0, keepdims=False)
        there = lax.dynamic_index_in_dim(padded, region + 1, 0, keepdims=False)
        near_pick = lax.dynamic_index_in_dim(near_table, region, 0, keepdims=False)[:, member, :]
        far_pick = lax.dynamic_index_in_dim(far_table, region, 0, keepdims=False)[:, member, :]
        fetched = jnp.concatenate([here[peer_index, near_pick], there[peer_index, far_pick]], 0).reshape(slot_count, 2, 3, 2 * F)
        begin = owner * PAIRS_DEV
        first_ids = lax.dynamic_slice_in_dim(first_slot, begin, PAIRS_DEV)
        second_ids = lax.dynamic_slice_in_dim(second_slot, begin, PAIRS_DEV)
        starts = lax.dynamic_slice_in_dim(window_start, begin, PAIRS_DEV)
        lengths = lax.dynamic_slice_in_dim(pair_delay_indices, begin, PAIRS_DEV)
        misfit, grad_first, grad_second = pair_terms(fetched[first_ids], fetched[second_ids], starts, lengths, lag_lookup_table)
        slot_grad = jax.ops.segment_sum(jnp.concatenate([grad_first, grad_second], 0), jnp.concatenate([first_ids, second_ids], 0), num_segments=slot_count).reshape(2, N_DEV, CAP, 3, 2 * F)
        totals = totals.at[region, peer_index, near_pick].add(slot_grad[0])
        totals = totals.at[region + 1, peer_index, far_pick].add(slot_grad[1])
        return (totals, misfit)
    start_totals = jnp.zeros((N_REGION + 1, N_DEV, RPD, 3, 2 * F), jnp.float32)
    totals, misfits = lax.scan(visit, start_totals, jnp.arange(DEVICES, dtype=jnp.int32))
    gathered = totals[:N_REGION].reshape(DEVICES, RPD * 3, 2 * F).astype(jnp.bfloat16)

    def reciprocal_factor(block):
        return lax.dot_general(block, forward, (((1,), (1,)), ((), ())), preferred_element_type=jnp.float32).astype(jnp.bfloat16)
    adjoint = lax.map(reciprocal_factor, gathered).reshape(STATION_TOTAL, 3, discrete_ticks)
    return (adjoint, misfits.reshape(PAIRS))
```

```python
import functools
import math

import jax
import jax.numpy as jnp
import ml_dtypes
import numpy as np
from jax import lax
from jax.experimental import pallas as pl
from jax.experimental.pallas import tpu as pltpu
from jax.sharding import PartitionSpec as P

F = 512
FLOW = 64
LAGS = 512
ZS = 8
YS = 4
CAP = 4
ROWS = 16
Q = 6
VMEM_BYTES = 40 * 1024 * 1024
BF = jnp.bfloat16
F32 = jnp.float32


def tables(ticks):
    rate = FLOW + np.arange(F, dtype=np.int64)
    turn = (np.arange(ticks, dtype=np.int64)[:, None] * rate[None, :]) % ticks
    angle = (turn.astype(np.float32) * np.float32(2.0 * math.pi / ticks)).astype(np.float64)
    forward = np.concatenate([np.cos(angle), -np.sin(angle)], 1).astype(np.float32)
    forward = (forward / np.float32(math.sqrt(ticks))).astype(ml_dtypes.bfloat16)
    shifts = np.arange(LAGS, dtype=np.int64) - LAGS // 2
    turn = (rate[:, None] * shifts[None, :]) % ticks
    angle = (turn.astype(np.float32) * np.float32(2.0 * math.pi / ticks)).astype(np.float64)
    lag = np.concatenate([np.cos(angle), -np.sin(angle)], 0).astype(np.float32)
    lag = (lag / np.float32(math.sqrt(F))).astype(ml_dtypes.bfloat16)
    return forward, lag


def z_pairs(step):
    return [(z * YS + y, (z + step) % ZS * YS + y) for z in range(ZS) for y in range(YS)]


def y_pairs(step, regions, shift):
    devs = ZS * YS
    return [
        (r * devs + z * YS + y, (r + shift) * devs + z * YS + (y + step) % YS)
        for r in range(max(0, -shift), min(regions, regions - shift))
        for z in range(ZS)
        for y in range(YS)
    ]


def iota(shape, axis):
    return lax.broadcasted_iota(jnp.int32, shape, axis)


def dot(a, b):
    return jnp.dot(a, b, preferred_element_type=F32)


def ring_place(offset):
    offset = lax.rem(offset + 2 * ZS, ZS)
    return jnp.where(offset == 0, 0, jnp.where(offset <= ZS // 2, 2 * offset - 1, 2 * (ZS - offset)))


def select_kernel(place_ref, *refs):
    blocks = refs[: ZS - 1]
    halves = refs[ZS - 1 : ZS + 1]
    near = refs[ZS + 1 : ZS + 1 + YS]
    far = refs[ZS + 1 + YS : ZS + 1 + 2 * YS]
    pick_out = refs[ZS + 1 + 2 * YS]
    z, y = place_ref[0], place_ref[1]
    split = halves[0].shape[0]

    def stacked(q):
        last = halves[0][q] if q < split else halves[1][q - split]
        return jnp.concatenate([block[q] for block in blocks] + [last], 0)

    total = 2 * YS * ZS * CAP
    wide = ZS * ROWS
    row = iota((total, 1), 0)
    cap, ring, step, side = row % CAP, row // CAP % ZS, row // (CAP * ZS) % YS, row // (CAP * ZS * YS)
    expand = (iota((total, wide), 1) == ring * ROWS).astype(BF)
    index = stacked(Q)[:, :total]
    spread = dot(expand, index)
    lane = side * (total // 2) + z * (YS * CAP) + (y + step) % YS * CAP + cap
    chosen = jnp.sum(jnp.where(iota((total, total), 1) == lane, spread, 0.0), 1, keepdims=True)
    target = ring * ROWS + chosen.astype(jnp.int32)
    pick = (iota((total, wide), 1) == target).astype(F32)
    pick_out[...] = pick.T.astype(BF)
    pick = pick.astype(BF)
    count = ZS * CAP
    for q in range(Q):
        got = dot(pick, stacked(q)).astype(BF)
        for k in range(YS):
            near[k][q // 3, q % 3] = got[k * count : (k + 1) * count]
            far[k][q // 3, q % 3] = got[(YS + k) * count : (YS + k + 1) * count]


def pair_kernel(column_ref, row_ref, lag_ref, *refs):
    slots = refs[: 2 * YS]
    misfit_ref = refs[2 * YS]
    outs = refs[2 * YS + 1 :]
    pairs = column_ref.shape[0]
    count = ZS * CAP
    near = YS * count
    lag = lag_ref[...]
    first = (iota((pairs, near), 1) == column_ref[:, 0:1]).astype(BF)
    second = (iota((pairs, 2 * near), 1) == column_ref[:, 1:2]).astype(BF)
    first_back = (iota((near, pairs), 0) == row_ref[0:1, :]).astype(BF)
    second_back = (iota((2 * near, pairs), 0) == row_ref[1:2, :]).astype(BF)

    def both(kind):
        spectra = jnp.concatenate([slot[kind, 0] for slot in slots], 0)
        a = dot(first, spectra[:near])
        b = dot(second, spectra)
        return a[:, :F], a[:, F:], b[:, :F], b[:, F:]

    ar, ai, br, bi = both(0)
    cr, ci, dr, di = both(1)
    real = (ar * br + ai * bi) - (cr * dr + ci * di)
    imag = (ai * br - ar * bi) - (ci * dr - cr * di)
    shifted = dot(real.astype(BF), lag[:F]) + dot(imag.astype(BF), lag[F:])
    position = iota((pairs, LAGS), 1)
    start = column_ref[:, 2:3]
    inside = (position >= start) & (position < start + column_ref[:, 3:4])
    residual = jnp.where(inside, shifted, 0.0)
    part = jnp.sum(residual * residual, axis=1, keepdims=True)

    @pl.when(pl.program_id(0) == 0)
    def _():
        misfit_ref[...] = jnp.zeros_like(misfit_ref)

    misfit_ref[...] += part * (1.0 / (2.0 * LAGS))
    slope = lax.dot_general(
        residual.astype(BF), lag, (((1,), (1,)), ((), ())), preferred_element_type=F32
    )
    gr, gi = slope[:, :F], slope[:, F:]
    grad_first = jnp.concatenate([gr * br - gi * bi, gr * bi + gi * br], 1).astype(BF)
    grad_second = jnp.concatenate([gr * ar + gi * ai, gr * ai - gi * ar], 1).astype(BF)
    total = dot(second_back, grad_second)
    top = total[:near] + dot(first_back, grad_first)
    for k in range(YS):
        outs[k][0] = top[k * count : (k + 1) * count].astype(BF)
        outs[YS + k][0] = total[near + k * count : near + (k + 1) * count].astype(BF)


def collect_kernel(place_ref, pick_ref, *refs):
    grads = refs[: 2 * YS]
    out = refs[2 * YS]
    z = place_ref[0]
    pick = pick_ref[...]
    for c in range(3):
        total = dot(pick, jnp.concatenate([grad[c] for grad in grads], 0)).astype(BF)
        for p in range(ZS):
            offset = (p + 1) // 2 if p % 2 else -(p // 2)
            out[lax.rem(z - offset + ZS, ZS), c] = total[p * ROWS : (p + 1) * ROWS]


def whole(count):
    return [pl.BlockSpec(memory_space=pltpu.VMEM)] * count


def on_device(
    regions,
    synthetic,
    observed,
    nearby_receiver_slots,
    far_rows,
    first_slot,
    second_slot,
    window_start,
    pair_delay_indices,
):
    ticks = synthetic.shape[2]
    pairs = first_slot.shape[0]
    forward_np, lag_np = tables(ticks)
    forward, lag = jnp.asarray(forward_np), jnp.asarray(lag_np)
    params = pltpu.CompilerParams(vmem_limit_bytes=VMEM_BYTES)
    scalars = pl.BlockSpec(memory_space=pltpu.SMEM)
    here = lax.axis_index("dev")
    z, y = here // YS, here % YS
    place = jnp.stack([z, y]).astype(jnp.int32)
    count = ZS * CAP

    far_index = lax.ppermute(far_rows, "region", [(r, r + 1) for r in range(regions - 1)])
    traces = jnp.stack([synthetic, observed]).transpose(0, 2, 1, 3).reshape(Q * ROWS, ticks)
    spectra = jnp.dot(traces, forward, preferred_element_type=F32).astype(BF).reshape(Q, ROWS, 2 * F)
    index = jnp.concatenate([nearby_receiver_slots.reshape(-1), far_index.reshape(-1)]).astype(BF)
    index = jnp.pad(index.reshape(1, 1, -1), ((0, 0), (0, ROWS - 1), (0, 2 * F - index.shape[0])))
    own = jnp.concatenate([spectra, index], 0)

    up = down = own
    blocks = [own]
    for _ in range(ZS // 2 - 1):
        up = lax.ppermute(up, "dev", z_pairs(1))
        down = lax.ppermute(down, "dev", z_pairs(-1))
        blocks += [up, down]
    split = (Q + 1) // 2
    halves = [
        lax.ppermute(up[:split], "dev", z_pairs(1)),
        lax.ppermute(down[split:], "dev", z_pairs(-1)),
    ]
    picked = pl.pallas_call(
        select_kernel,
        out_shape=[jax.ShapeDtypeStruct((2, 3, count, 2 * F), BF)] * (2 * YS)
        + [jax.ShapeDtypeStruct((ZS * ROWS, 2 * YS * count), BF)],
        in_specs=[scalars] + whole(ZS + 1),
        out_specs=whole(2 * YS + 1),
        compiler_params=params,
    )(place, *blocks, *halves)
    pick = picked[-1]
    slots = [picked[0]]
    slots += [
        lax.ppermute(picked[k], ("region", "dev"), y_pairs(k, regions, 0)) for k in range(1, YS)
    ]
    slots += [
        lax.ppermute(picked[YS + k], ("region", "dev"), y_pairs(k, regions, -1)) for k in range(YS)
    ]

    def moved(slot):
        side, member, cap = slot // (ZS * YS * CAP), slot // CAP % (ZS * YS), slot % CAP
        step = lax.rem(y - member % YS + YS, YS)
        ring = ring_place(z - member // YS)
        return ((side * YS + step) * ZS + ring) * CAP + cap

    first, second = moved(first_slot), moved(second_slot)
    column = jnp.stack([first, second, window_start, pair_delay_indices], 1)
    row = jnp.stack([first, second])
    results = pl.pallas_call(
        pair_kernel,
        grid=(3,),
        out_shape=[jax.ShapeDtypeStruct((pairs, 1), F32)]
        + [jax.ShapeDtypeStruct((3, count, 2 * F), BF)] * (2 * YS),
        in_specs=[
            pl.BlockSpec((pairs, 4), lambda c: (0, 0)),
            pl.BlockSpec((2, pairs), lambda c: (0, 0)),
            pl.BlockSpec((2 * F, LAGS), lambda c: (0, 0)),
        ]
        + [pl.BlockSpec((2, 1, count, 2 * F), lambda c: (0, c, 0, 0))] * (2 * YS),
        out_specs=[pl.BlockSpec((pairs, 1), lambda c: (0, 0))]
        + [pl.BlockSpec((1, count, 2 * F), lambda c: (c, 0, 0))] * (2 * YS),
        compiler_params=params,
    )(column, row, lag, *slots)
    misfit, grads = results[0].reshape(pairs), results[1:]
    back = [grads[0]]
    back += [
        lax.ppermute(grads[k], ("region", "dev"), y_pairs(-k, regions, 0)) for k in range(1, YS)
    ]
    back += [
        lax.ppermute(grads[YS + k], ("region", "dev"), y_pairs(-k, regions, 1)) for k in range(YS)
    ]
    sums = pl.pallas_call(
        collect_kernel,
        out_shape=jax.ShapeDtypeStruct((ZS, 3, ROWS, 2 * F), BF),
        in_specs=[scalars] + whole(2 * YS + 1),
        out_specs=pl.BlockSpec(memory_space=pltpu.VMEM),
        compiler_params=params,
    )(place, pick, *back)
    groups = [[z * YS + y for z in range(ZS)] for y in range(YS)]
    parts = lax.all_to_all(
        sums, "dev", split_axis=0, concat_axis=0, tiled=True, axis_index_groups=groups
    )
    total = jnp.sum(parts.astype(F32), 0).astype(BF).reshape(3 * ROWS, 2 * F)
    adjoint = lax.dot_general(
        total, forward, (((1,), (1,)), ((), ())), preferred_element_type=F32
    )
    adjoint = adjoint.astype(BF).reshape(3, ROWS, ticks).transpose(1, 0, 2)
    return (adjoint, misfit)


def solution(mesh):
    both = ("region", "dev")
    placed = (P(both, None, None),) * 2 + (P(both, None),) * 2 + (P(both),) * 4
    return jax.shard_map(
        functools.partial(on_device, mesh.shape["region"]),
        mesh=mesh,
        in_specs=placed,
        out_specs=(P(both, None, None), P(both)),
        check_vma=False,
    )
```

```python
import functools
import math

import jax
import jax.numpy as jnp
import ml_dtypes
import numpy as np
from jax import lax
from jax.experimental import pallas as pl
from jax.experimental.pallas import tpu as pltpu
from jax.sharding import PartitionSpec as P

F = 512
FLOW = 64
LAGS = 512
ZS = 8
YS = 4
CAP = 4
ROWS = 16
Q = 6
RADIX = 4
EARLY, LATE = (0, 1, 2, 3), (4, 5, 6, 7)
VMEM_BYTES = 40 * 1024 * 1024
BF = jnp.bfloat16
F32 = jnp.float32


def tables(ticks):
    rate = FLOW + np.arange(F, dtype=np.int64).reshape(-1, RADIX).T.reshape(-1)
    quarter = ticks // RADIX
    turn = (np.arange(quarter, dtype=np.int64)[:, None] * rate[None, :]) % ticks
    angle = (turn.astype(np.float32) * np.float32(2.0 * math.pi / ticks)).astype(np.float64)
    forward = np.stack([np.cos(angle), -np.sin(angle)], 1).astype(np.float32)
    forward = (forward / np.float32(math.sqrt(ticks))).astype(ml_dtypes.bfloat16)
    forward = forward.reshape(quarter, 2, RADIX, F // RADIX).transpose(2, 0, 1, 3)
    forward = forward.reshape(RADIX, quarter, 2 * F // RADIX)
    shifts = np.arange(LAGS, dtype=np.int64) - LAGS // 2
    turn = (rate[:, None] * shifts[None, :]) % ticks
    angle = (turn.astype(np.float32) * np.float32(2.0 * math.pi / ticks)).astype(np.float64)
    lag = np.concatenate([np.cos(angle), -np.sin(angle)], 0).astype(np.float32)
    lag = (lag / np.float32(math.sqrt(F))).astype(ml_dtypes.bfloat16)
    return forward, np.ascontiguousarray(forward.transpose(0, 2, 1)), lag


def z_pairs(step):
    return [(z * YS + y, (z + step) % ZS * YS + y) for z in range(ZS) for y in range(YS)]


def y_pairs(step, regions, shift):
    devs = ZS * YS
    return [
        (r * devs + z * YS + y, (r + shift) * devs + z * YS + (y + step) % YS)
        for r in range(max(0, -shift), min(regions, regions - shift))
        for z in range(ZS)
        for y in range(YS)
    ]


def iota(shape, axis):
    return lax.broadcasted_iota(jnp.int32, shape, axis)


def dot(a, b):
    return jnp.dot(a, b, preferred_element_type=F32)


def forward_kernel(synthetic_ref, observed_ref, table_ref, out_ref):
    quarter = synthetic_ref.shape[2] // RADIX
    group = F // RADIX
    out_ref[Q] = jnp.zeros((ROWS, 2 * F), BF)
    traces = [ref[c] for ref in (synthetic_ref, observed_ref) for c in range(3)]
    traces = jnp.concatenate(traces, 0)
    for c in range(RADIX):
        sums = [dot(traces[:, j * quarter : (j + 1) * quarter], table_ref[c]) for j in range(RADIX)]
        (r0, i0), (r1, i1), (r2, i2), (r3, i3) = [(p[:, :group], p[:, group:]) for p in sums]
        if c == 0:
            real, imag = (r0 + r1) + (r2 + r3), (i0 + i1) + (i2 + i3)
        elif c == 1:
            real, imag = (r0 - r2) + (i1 - i3), (i0 - i2) - (r1 - r3)
        elif c == 2:
            real, imag = (r0 - r1) + (r2 - r3), (i0 - i1) + (i2 - i3)
        else:
            real, imag = (r0 - r2) - (i1 - i3), (i0 - i2) + (r1 - r3)
        at = c * group
        out_ref[:Q, :, at : at + group] = real.astype(BF).reshape(Q, ROWS, group)
        out_ref[:Q, :, F + at : F + at + group] = imag.astype(BF).reshape(Q, ROWS, group)


def inverse_kernel(near_ref, far_ref, table_ref, out_ref):
    rows = out_ref.shape[0]
    quarter = out_ref.shape[1] // RADIX
    part = table_ref.shape[2]
    group = F // RADIX
    total = (near_ref[...] + far_ref[...]).astype(BF)
    real = [total[:, c * group : (c + 1) * group] for c in range(RADIX)]
    imag = [total[:, F + c * group : F + (c + 1) * group] for c in range(RADIX)]
    plain = [jnp.concatenate([real[c], imag[c]], 1) for c in range(RADIX)]
    turned = [jnp.concatenate([-imag[c], real[c]], 1) for c in range(RADIX)]
    p0, p2 = dot(plain[0], table_ref[0]), dot(plain[2], table_ref[2])
    one = dot(jnp.concatenate([plain[1], turned[1]], 0), table_ref[1])
    three = dot(jnp.concatenate([plain[3], turned[3]], 0), table_ref[3])
    p1, q1, p3, q3 = one[:rows], one[rows:], three[:rows], three[rows:]
    parts = (p0 + p2) + (p1 + p3), (p0 - p2) + (q1 - q3), (p0 + p2) - (p1 + p3), (p0 - p2) - (q1 - q3)
    start = pl.program_id(0) * part
    for j, value in enumerate(parts):
        at = pl.multiple_of(start + j * quarter, part)
        out_ref[:, pl.ds(at, part)] = value.astype(BF)


def position():
    here = lax.axis_index("dev")
    return here // YS, here % YS


def select_kernel(jobs, places, *refs):
    blocks, outs = dict(zip(places, refs)), refs[len(places) :]
    z, y = position()
    for n, (side, ring) in enumerate(jobs):
        out, size = outs[n * YS : (n + 1) * YS], len(ring)
        count, wide = size * CAP, size * ROWS
        row = iota((YS * count, 1), 0)
        cap, block, step = row % CAP, row // CAP % size, row // count
        expand = (iota((YS * count, wide), 1) == block * ROWS + side * CAP + cap).astype(BF)
        index = jnp.concatenate([blocks[p][Q, :, : 4 * ZS * YS] for p in ring], 0)
        spread = dot(expand, index)
        lane = z * YS + (y + step) % YS
        value = jnp.sum(jnp.where(iota(spread.shape, 1) == lane, spread, 0.0), 1, keepdims=True)
        pick = iota((YS * count, wide), 1) == block * ROWS + value.astype(jnp.int32)
        pick = pick.astype(BF)
        for q in range(Q):
            got = dot(pick, jnp.concatenate([blocks[p][q] for p in ring], 0)).astype(BF)
            for k in range(YS):
                out[k][q // 3, q % 3] = got[k * count : (k + 1) * count]


def ring_place(offset):
    offset = offset % ZS
    return jnp.where(offset == 0, 0, jnp.where(offset <= ZS // 2, 2 * offset - 1, 2 * (ZS - offset)))


def pair_kernel(slots_ref, lag_ref, *refs):
    pieces, (misfit_ref, out_ref) = refs[:-2], refs[-2:]
    pairs = slots_ref.shape[1]
    peers = ZS * YS
    near = peers * CAP
    z, y = position()
    lag = lag_ref[...]
    slots = slots_ref[:2]
    side, member, cap = slots // near, slots // CAP % peers, slots % CAP
    step = (y - member % YS + YS) % YS
    held = ((side * YS + step) * ZS + ring_place(z - member // YS + ZS)) * CAP + cap
    back = (member * 2 + side) * CAP + cap
    first_back = (iota((2 * near, pairs), 0) == back[:1]).astype(BF)
    second_back = (iota((2 * near, pairs), 0) == back[1:]).astype(BF)
    column = jnp.concatenate([held, slots_ref[2:4], held, held], 0).astype(F32).T.astype(jnp.int32)
    first = (iota((pairs, near), 1) == column[:, 0:1]).astype(BF)
    second = (iota((pairs, 2 * near), 1) == column[:, 1:2]).astype(BF)

    def both(kind):
        spectra = jnp.concatenate([piece[kind, 0] for piece in pieces], 0)
        a = dot(first, spectra[:near])
        b = dot(second, spectra)
        return a[:, :F], a[:, F:], b[:, :F], b[:, F:]

    ar, ai, br, bi = both(0)
    cr, ci, dr, di = both(1)
    real = (ar * br + ai * bi) - (cr * dr + ci * di)
    imag = (ai * br - ar * bi) - (ci * dr - cr * di)
    shifted = dot(real.astype(BF), lag[:F]) + dot(imag.astype(BF), lag[F:])
    at = iota((pairs, LAGS), 1)
    start = column[:, 2:3]
    inside = (at >= start) & (at < start + column[:, 3:4])
    residual = jnp.where(inside, shifted, 0.0)
    part = jnp.sum(residual * residual, axis=1, keepdims=True)

    @pl.when(pl.program_id(0) == 0)
    def _():
        misfit_ref[...] = jnp.zeros_like(misfit_ref)

    misfit_ref[...] += part * (1.0 / (2.0 * LAGS))
    slope = lax.dot_general(
        residual.astype(BF), lag, (((1,), (1,)), ((), ())), preferred_element_type=F32
    )
    gr, gi = slope[:, :F], slope[:, F:]
    grad_first = jnp.concatenate([gr * br - gi * bi, gr * bi + gi * br], 1).astype(BF)
    grad_second = jnp.concatenate([gr * ar + gi * ai, gr * ai - gi * ar], 1).astype(BF)
    total = dot(first_back, grad_first) + dot(second_back, grad_second)
    total = total.reshape(peers, 2 * CAP, 2 * F)
    out_ref[...] = jnp.concatenate([total[..., :F], total[..., F:]], 1).astype(BF)


def collect_kernel(held_ref, grad_ref, near_ref, far_ref):
    rows = held_ref.shape[1]
    pick = (iota((4 * ROWS, rows), 0) == held_ref[...]).astype(BF)
    total = dot(pick, grad_ref[...].reshape(rows, F))
    near_ref[...] = jnp.concatenate([total[:ROWS], total[2 * ROWS : 3 * ROWS]], 1)
    far_ref[...] = jnp.concatenate([total[ROWS : 2 * ROWS], total[3 * ROWS :]], 1)


def whole(count):
    return [pl.BlockSpec(memory_space=pltpu.VMEM)] * count


def shape(dims, kind=BF):
    return jax.ShapeDtypeStruct(dims, kind)


def cost(flops, size):
    return pl.CostEstimate(flops=flops, bytes_accessed=size, transcendentals=0)


def on_device(
    regions,
    synthetic,
    observed,
    nearby_receiver_slots,
    far_rows,
    first_slot,
    second_slot,
    window_start,
    pair_delay_indices,
):
    ticks = synthetic.shape[2]
    pairs = first_slot.shape[0]
    forward, inverse, lag = [jnp.asarray(table) for table in tables(ticks)]
    params = pltpu.CompilerParams(vmem_limit_bytes=VMEM_BYTES)
    peers = ZS * YS

    def z_move(value, step):
        return lax.ppermute(value, "dev", z_pairs(step))

    def y_move(value, step, shift):
        return lax.ppermute(value, ("region", "dev"), y_pairs(step, regions, shift))

    far_index = lax.ppermute(far_rows.T, "region", [(r, r + 1) for r in range(regions - 1)])
    sources = [synthetic.transpose(1, 0, 2), observed.transpose(1, 0, 2)]
    own = pl.pallas_call(
        forward_kernel,
        grid=(1,),
        out_shape=shape((Q + 1, ROWS, 2 * F)),
        in_specs=[pl.BlockSpec((3, ROWS, ticks), lambda i: (0, 0, 0))] * 2
        + [pl.BlockSpec(forward.shape, lambda i: (0, 0, 0))],
        out_specs=pl.BlockSpec((Q + 1, ROWS, 2 * F), lambda i: (0, 0, 0)),
        compiler_params=pltpu.CompilerParams(vmem_limit_bytes=60 * 1024 * 1024),
        cost_estimate=cost(2 * Q * ROWS * ticks * 2 * F, 3 << 20),
    )(*sources, forward)
    index = jnp.concatenate([nearby_receiver_slots.T, far_index]).astype(BF)
    index = jnp.pad(index, ((0, ROWS - index.shape[0]), (0, 2 * F - index.shape[1])))
    own = lax.dynamic_update_slice(own, index[None], (Q, 0, 0))

    def select(jobs, blocks):
        sizes = [len(ring) * CAP for _, ring in jobs for _ in range(YS)]
        return pl.pallas_call(
            functools.partial(select_kernel, jobs, tuple(blocks)),
            out_shape=[shape((2, 3, size, 2 * F)) for size in sizes],
            in_specs=whole(len(blocks)),
            out_specs=whole(len(sizes)),
            compiler_params=params,
            cost_estimate=cost(1 << 29, 5 << 20),
        )(*blocks.values())

    up, down = z_move(own, 1), z_move(own, -1)
    up2, down2 = z_move(up, 1), z_move(down, -1)
    up3, down3 = z_move(up2, 1), z_move(down2, -1)
    early = select([(0, EARLY)], dict(zip(EARLY, [own, up, down, up2])))
    early = [early[0]] + [y_move(early[k], k, 0) for k in range(1, YS)]
    split = Q // 2
    half_up, half_down = up3[:split], down3[split:]
    half_up, early[0] = lax.optimization_barrier((half_up, early[0]))
    last = jnp.concatenate([z_move(half_up, 1), z_move(half_down, -1)], 0)
    blocks = dict(enumerate([own, up, down, up2, down2, up3, down3, last]))
    late = select([(0, LATE), (1, EARLY + LATE)], blocks)
    far = [y_move(piece, k, -1) for k, piece in enumerate(late[YS:])]
    late = [late[0]] + [y_move(late[k], k, 0) for k in range(1, YS)]
    pieces = [piece for pair in zip(early, late) for piece in pair] + far
    slots = jnp.stack([first_slot, second_slot, window_start, pair_delay_indices])
    misfit, grads = pl.pallas_call(
        pair_kernel,
        grid=(3,),
        out_shape=[shape((pairs, 1), F32), shape((peers, 3 * ROWS, F))],
        in_specs=[
            pl.BlockSpec((4, pairs), lambda c: (0, 0)),
            pl.BlockSpec((2 * F, LAGS), lambda c: (0, 0)),
        ]
        + [
            pl.BlockSpec((2, 1) + piece.shape[2:], lambda c: (0, c, 0, 0)) for piece in pieces
        ],
        out_specs=[
            pl.BlockSpec((pairs, 1), lambda c: (0, 0)),
            pl.BlockSpec((peers, ROWS, F), lambda c: (0, c, 0)),
        ],
        compiler_params=params,
        cost_estimate=cost(9 << 30, 9 << 20),
    )(slots, lag, *pieces)
    grads = lax.all_to_all(grads, "dev", split_axis=0, concat_axis=0, tiled=True)
    held = jnp.concatenate([nearby_receiver_slots, far_rows + ROWS], 1)
    held = jnp.concatenate([held, held + 2 * ROWS], 1).reshape(1, peers * ROWS)
    near_sum, far_sum = pl.pallas_call(
        collect_kernel,
        grid=(3,),
        out_shape=[shape((3 * ROWS, 2 * F), F32)] * 2,
        in_specs=[
            pl.BlockSpec((1, peers * ROWS), lambda c: (0, 0)),
            pl.BlockSpec((peers, ROWS, F), lambda c: (0, c, 0)),
        ],
        out_specs=[pl.BlockSpec((ROWS, 2 * F), lambda c: (c, 0))] * 2,
        compiler_params=params,
        cost_estimate=cost(1 << 26, 2 << 20),
    )(held, grads)
    far_sum = lax.ppermute(far_sum, "region", [(r, r + 1) for r in range(regions - 1)])
    part = ticks // RADIX // 2
    adjoint = pl.pallas_call(
        inverse_kernel,
        grid=(2,),
        out_shape=shape((3 * ROWS, ticks)),
        in_specs=[pl.BlockSpec((3 * ROWS, 2 * F), lambda i: (0, 0))] * 2
        + [pl.BlockSpec((RADIX, 2 * F // RADIX, part), lambda i: (0, 0, i))],
        out_specs=pl.BlockSpec((3 * ROWS, ticks), lambda i: (0, 0)),
        compiler_params=pltpu.CompilerParams(vmem_limit_bytes=60 * 1024 * 1024),
        cost_estimate=cost(2 * 3 * ROWS * ticks * 2 * F, 3 << 20),
    )(near_sum, far_sum, inverse)
    adjoint = adjoint.reshape(3, ROWS, ticks).transpose(1, 0, 2)
    return (adjoint, misfit.reshape(pairs))


def solution(mesh):
    both = ("region", "dev")
    placed = (P(both, None, None),) * 2 + (P(both, None),) * 2 + (P(both),) * 4
    return jax.shard_map(
        functools.partial(on_device, mesh.shape["region"]),
        mesh=mesh,
        in_specs=placed,
        out_specs=(P(both, None, None), P(both)),
        check_vma=False,
    )
```

```python
import functools
import math

import jax
import jax.numpy as jnp
import ml_dtypes
import numpy as np
from jax import lax
from jax.experimental import pallas as pl
from jax.experimental.pallas import tpu as pltpu
from jax.sharding import PartitionSpec as P

F = 512
FLOW = 64
LAGS = 512
ZS = 8
YS = 4
CAP = 4
ROWS = 16
Q = 6
RADIX = 4
EARLY, LATE = (0, 1, 2, 3), (4, 5, 6, 7)
VMEM_BYTES = 40 * 1024 * 1024
BF = jnp.bfloat16
F32 = jnp.float32


def tables(ticks):
    rate = FLOW + np.arange(F, dtype=np.int64).reshape(-1, RADIX).T.reshape(-1)
    quarter = ticks // RADIX
    turn = (np.arange(quarter, dtype=np.int64)[:, None] * rate[None, :]) % ticks
    angle = (turn.astype(np.float32) * np.float32(2.0 * math.pi / ticks)).astype(np.float64)
    forward = np.stack([np.cos(angle), -np.sin(angle)], 1).astype(np.float32)
    forward = (forward / np.float32(math.sqrt(ticks))).astype(ml_dtypes.bfloat16)
    forward = forward.reshape(quarter, 2, RADIX, F // RADIX).transpose(2, 0, 1, 3)
    forward = forward.reshape(RADIX, quarter, 2 * F // RADIX)
    shifts = np.arange(LAGS, dtype=np.int64) - LAGS // 2
    turn = (rate[:, None] * shifts[None, :]) % ticks
    angle = (turn.astype(np.float32) * np.float32(2.0 * math.pi / ticks)).astype(np.float64)
    lag = np.concatenate([np.cos(angle), -np.sin(angle)], 0).astype(np.float32)
    lag = (lag / np.float32(math.sqrt(F))).astype(ml_dtypes.bfloat16)
    return forward, np.ascontiguousarray(forward.transpose(0, 2, 1)), lag


def z_pairs(step):
    return [(z * YS + y, (z + step) % ZS * YS + y) for z in range(ZS) for y in range(YS)]


def y_pairs(step, regions, shift):
    devs = ZS * YS
    return [
        (r * devs + z * YS + y, (r + shift) * devs + z * YS + (y + step) % YS)
        for r in range(max(0, -shift), min(regions, regions - shift))
        for z in range(ZS)
        for y in range(YS)
    ]


def iota(shape, axis):
    return lax.broadcasted_iota(jnp.int32, shape, axis)


def dot(a, b):
    return jnp.dot(a, b, preferred_element_type=F32)


def forward_kernel(synthetic_ref, observed_ref, far_table_ref, out_ref, held, table_ref, done):
    quarter = synthetic_ref.shape[2] // RADIX
    group = F // RADIX
    copies = [
        pltpu.make_async_copy(ref, held.at[n], done.at[n])
        for n, ref in enumerate((synthetic_ref, observed_ref))
    ]
    copies += [
        pltpu.make_async_copy(far_table_ref.at[c], table_ref.at[c], done.at[2 + c])
        for c in range(RADIX)
    ]
    for copy in copies:
        copy.start()
    copies[0].wait()
    copies[1].wait()
    traces = jnp.concatenate([held[n, c] for n in range(2) for c in range(3)], 0)
    for c in range(RADIX):
        copies[2 + c].wait()
        sums = [dot(traces[:, j * quarter : (j + 1) * quarter], table_ref[c]) for j in range(RADIX)]
        (r0, i0), (r1, i1), (r2, i2), (r3, i3) = [(p[:, :group], p[:, group:]) for p in sums]
        if c == 0:
            real, imag = (r0 + r1) + (r2 + r3), (i0 + i1) + (i2 + i3)
        elif c == 1:
            real, imag = (r0 - r2) + (i1 - i3), (i0 - i2) - (r1 - r3)
        elif c == 2:
            real, imag = (r0 - r1) + (r2 - r3), (i0 - i1) + (i2 - i3)
        else:
            real, imag = (r0 - r2) - (i1 - i3), (i0 - i2) + (r1 - r3)
        at = c * group
        out_ref[:Q, :, at : at + group] = real.astype(BF).reshape(Q, ROWS, group)
        out_ref[:Q, :, F + at : F + at + group] = imag.astype(BF).reshape(Q, ROWS, group)


def index_kernel(near_ref, far_ref, _, out_ref):
    cap, peers = near_ref.shape
    both = jnp.concatenate([near_ref[...], far_ref[...]], 0).astype(F32)
    both = jnp.concatenate([both, jnp.zeros((2 * cap, 4 * peers - peers), F32)], 1)
    out_ref[Q, :, : 4 * peers] = jnp.concatenate([both, jnp.zeros_like(both)], 0).astype(BF)


def fetch_kernel(source_ref, _, out_ref, done):
    copy = pltpu.make_async_copy(source_ref, out_ref, done)
    copy.start()
    copy.wait()


def inverse_kernel(near_ref, far_ref, table_ref, out_ref):
    rows = out_ref.shape[0]
    quarter = out_ref.shape[1] // RADIX
    group = F // RADIX
    total = (near_ref[...] + far_ref[...].astype(F32)).astype(BF)
    real = [total[:, c * group : (c + 1) * group] for c in range(RADIX)]
    imag = [total[:, F + c * group : F + (c + 1) * group] for c in range(RADIX)]
    plain = [jnp.concatenate([real[c], imag[c]], 1) for c in range(RADIX)]
    turned = [jnp.concatenate([-imag[c], real[c]], 1) for c in range(RADIX)]
    p0, p2 = dot(plain[0], table_ref[0]), dot(plain[2], table_ref[2])
    one = dot(jnp.concatenate([plain[1], turned[1]], 0), table_ref[1])
    three = dot(jnp.concatenate([plain[3], turned[3]], 0), table_ref[3])
    p1, q1, p3, q3 = one[:rows], one[rows:], three[:rows], three[rows:]
    out_ref[:, :quarter] = ((p0 + p2) + (p1 + p3)).astype(BF)
    out_ref[:, quarter : 2 * quarter] = ((p0 - p2) + (q1 - q3)).astype(BF)
    out_ref[:, 2 * quarter : 3 * quarter] = ((p0 + p2) - (p1 + p3)).astype(BF)
    out_ref[:, 3 * quarter :] = ((p0 - p2) - (q1 - q3)).astype(BF)


def position():
    here = lax.axis_index("dev")
    return here // YS, here % YS


def select_kernel(jobs, places, *refs):
    blocks, outs = dict(zip(places, refs)), refs[len(places) :]
    z, y = position()
    for n, (side, ring) in enumerate(jobs):
        out, size = outs[n * YS : (n + 1) * YS], len(ring)
        count, wide = size * CAP, size * ROWS
        row = iota((YS * count, 1), 0)
        cap, block, step = row % CAP, row // CAP % size, row // count
        expand = (iota((YS * count, wide), 1) == block * ROWS + side * CAP + cap).astype(BF)
        index = jnp.concatenate([blocks[p][Q, :, : 4 * ZS * YS] for p in ring], 0)
        spread = dot(expand, index)
        lane = z * YS + (y + step) % YS
        value = jnp.sum(jnp.where(iota(spread.shape, 1) == lane, spread, 0.0), 1, keepdims=True)
        pick = iota((YS * count, wide), 1) == block * ROWS + value.astype(jnp.int32)
        pick = pick.astype(BF)
        for q in range(Q):
            got = dot(pick, jnp.concatenate([blocks[p][q] for p in ring], 0)).astype(BF)
            for k in range(YS):
                out[k][q // 3, q % 3] = got[k * count : (k + 1) * count]


def ring_place(offset):
    offset = offset % ZS
    return jnp.where(offset == 0, 0, jnp.where(offset <= ZS // 2, 2 * offset - 1, 2 * (ZS - offset)))


def pair_kernel(slots_ref, lag_ref, *refs):
    pieces, (misfit_ref, out_ref) = refs[:-2], refs[-2:]
    pairs = slots_ref.shape[1]
    peers = ZS * YS
    near = peers * CAP
    z, y = position()
    lag = lag_ref[...]
    slots = slots_ref[:2]
    side, member, cap = slots // near, slots // CAP % peers, slots % CAP
    step = (y - member % YS + YS) % YS
    held = ((side * YS + step) * ZS + ring_place(z - member // YS + ZS)) * CAP + cap
    back = (member * 2 + side) * CAP + cap
    first_back = (iota((2 * near, pairs), 0) == back[:1]).astype(BF)
    second_back = (iota((2 * near, pairs), 0) == back[1:]).astype(BF)
    column = jnp.concatenate([held, slots_ref[2:4], held, held], 0).astype(F32).T.astype(jnp.int32)
    first = (iota((pairs, near), 1) == column[:, 0:1]).astype(BF)
    second = (iota((pairs, 2 * near), 1) == column[:, 1:2]).astype(BF)

    def both(kind):
        spectra = jnp.concatenate([piece[kind, 0] for piece in pieces], 0)
        a = dot(first, spectra[:near])
        b = dot(second, spectra)
        return a[:, :F], a[:, F:], b[:, :F], b[:, F:]

    ar, ai, br, bi = both(0)
    cr, ci, dr, di = both(1)
    real = (ar * br + ai * bi) - (cr * dr + ci * di)
    imag = (ai * br - ar * bi) - (ci * dr - cr * di)
    shifted = dot(real.astype(BF), lag[:F]) + dot(imag.astype(BF), lag[F:])
    at = iota((pairs, LAGS), 1)
    start = column[:, 2:3]
    inside = (at >= start) & (at < start + column[:, 3:4])
    residual = jnp.where(inside, shifted, 0.0)
    part = jnp.sum(residual * residual, axis=1, keepdims=True)

    @pl.when(pl.program_id(0) == 0)
    def _():
        misfit_ref[...] = jnp.zeros_like(misfit_ref)

    misfit_ref[...] += part * (1.0 / (2.0 * LAGS))
    slope = lax.dot_general(
        residual.astype(BF), lag, (((1,), (1,)), ((), ())), preferred_element_type=F32
    )
    gr, gi = slope[:, :F], slope[:, F:]
    grad_first = jnp.concatenate([gr * br - gi * bi, gr * bi + gi * br], 1).astype(BF)
    grad_second = jnp.concatenate([gr * ar + gi * ai, gr * ai - gi * ar], 1).astype(BF)
    total = dot(first_back, grad_first) + dot(second_back, grad_second)
    total = total.reshape(peers, 2 * CAP, 2 * F)
    out_ref[...] = jnp.concatenate([total[..., :F], total[..., F:]], 1).astype(BF)


def collect_kernel(held_ref, grad_ref, near_ref, far_ref):
    rows = held_ref.shape[1]
    pick = (iota((4 * ROWS, rows), 0) == held_ref[...]).astype(BF)
    total = dot(pick, grad_ref[...].reshape(rows, F))
    near_ref[...] = jnp.concatenate([total[:ROWS], total[2 * ROWS : 3 * ROWS]], 1)
    far_ref[...] = jnp.concatenate([total[ROWS : 2 * ROWS], total[3 * ROWS :]], 1).astype(BF)


def whole(count):
    return [pl.BlockSpec(memory_space=pltpu.VMEM)] * count


def shape(dims, kind=BF):
    return jax.ShapeDtypeStruct(dims, kind)


def cost(flops, size):
    return pl.CostEstimate(flops=flops, bytes_accessed=size, transcendentals=0)


def on_device(
    regions,
    synthetic,
    observed,
    nearby_receiver_slots,
    far_rows,
    first_slot,
    second_slot,
    window_start,
    pair_delay_indices,
):
    ticks = synthetic.shape[2]
    pairs = first_slot.shape[0]
    forward, inverse, lag = [jnp.asarray(table) for table in tables(ticks)]
    params = pltpu.CompilerParams(vmem_limit_bytes=VMEM_BYTES)
    peers = ZS * YS

    def z_move(value, step):
        return lax.ppermute(value, "dev", z_pairs(step))

    def y_move(value, step, shift):
        return lax.ppermute(value, ("region", "dev"), y_pairs(step, regions, shift))

    far_index = lax.ppermute(far_rows.T, "region", [(r, r + 1) for r in range(regions - 1)])
    sources = [synthetic.transpose(1, 0, 2), observed.transpose(1, 0, 2)]
    own = pl.pallas_call(
        forward_kernel,
        out_shape=shape((Q + 1, ROWS, 2 * F)),
        in_specs=[pl.BlockSpec(memory_space=pl.ANY)] * 3,
        out_specs=whole(1)[0],
        scratch_shapes=[
            pltpu.VMEM((2, 3, ROWS, ticks), BF),
            pltpu.VMEM(forward.shape, BF),
            pltpu.SemaphoreType.DMA((2 + RADIX,)),
        ],
        compiler_params=pltpu.CompilerParams(vmem_limit_bytes=63_225_856),
        cost_estimate=cost(2 * Q * ROWS * ticks * 2 * F, 3 << 20),
    )(*sources, forward)
    own = pl.pallas_call(
        index_kernel,
        out_shape=shape(own.shape),
        in_specs=whole(3),
        out_specs=whole(1)[0],
        input_output_aliases={2: 0},
        compiler_params=pltpu.CompilerParams(vmem_limit_bytes=VMEM_BYTES // 2),
        cost_estimate=cost(1 << 20, 1 << 16),
    )(nearby_receiver_slots.T, far_index, own)

    def select(jobs, blocks):
        sizes = [len(ring) * CAP for _, ring in jobs for _ in range(YS)]
        return pl.pallas_call(
            functools.partial(select_kernel, jobs, tuple(blocks)),
            out_shape=[shape((2, 3, size, 2 * F)) for size in sizes],
            in_specs=whole(len(blocks)),
            out_specs=whole(len(sizes)),
            compiler_params=params,
            cost_estimate=cost(1 << 29, 5 << 20),
        )(*blocks.values())

    up, down = z_move(own, 1), z_move(own, -1)
    up2, down2 = z_move(up, 1), z_move(down, -1)
    up3, down3 = z_move(up2, 1), z_move(down2, -1)
    early = select([(0, EARLY)], dict(zip(EARLY, [own, up, down, up2])))
    early = [early[0]] + [y_move(early[k], k, 0) for k in range(1, YS)]
    split = Q // 2
    half_up, half_down = up3[:split], down3[split:]
    half_up, early[0] = lax.optimization_barrier((half_up, early[0]))
    last = jnp.concatenate([z_move(half_up, 1), z_move(half_down, -1)], 0)
    blocks = dict(enumerate([own, up, down, up2, down2, up3, down3, last]))
    late = select([(0, LATE), (1, EARLY + LATE)], blocks)
    far = [y_move(piece, k, -1) for k, piece in enumerate(late[YS:])]
    late = [late[0]] + [y_move(late[k], k, 0) for k in range(1, YS)]
    pieces = [piece for pair in zip(early, late) for piece in pair] + far
    slots = jnp.stack([first_slot, second_slot, window_start, pair_delay_indices])
    misfit, grads = pl.pallas_call(
        pair_kernel,
        grid=(3,),
        out_shape=[shape((pairs, 1), F32), shape((peers, 3 * ROWS, F))],
        in_specs=[
            pl.BlockSpec((4, pairs), lambda c: (0, 0)),
            pl.BlockSpec((2 * F, LAGS), lambda c: (0, 0)),
        ]
        + [
            pl.BlockSpec((2, 1) + piece.shape[2:], lambda c: (0, c, 0, 0)) for piece in pieces
        ],
        out_specs=[
            pl.BlockSpec((pairs, 1), lambda c: (0, 0)),
            pl.BlockSpec((peers, ROWS, F), lambda c: (0, c, 0)),
        ],
        compiler_params=params,
        cost_estimate=cost(9 << 30, 9 << 20),
    )(slots, lag, *pieces)
    grads = lax.all_to_all(grads, "dev", split_axis=0, concat_axis=0, tiled=True)
    grads, misfit = lax.optimization_barrier((grads, misfit.reshape(pairs)))
    held = jnp.concatenate([nearby_receiver_slots, far_rows + ROWS], 1)
    held = jnp.concatenate([held, held + 2 * ROWS], 1).reshape(1, peers * ROWS)
    near_sum, far_sum = pl.pallas_call(
        collect_kernel,
        grid=(3,),
        out_shape=[shape((3 * ROWS, 2 * F), F32), shape((3 * ROWS, 2 * F))],
        in_specs=[
            pl.BlockSpec((1, peers * ROWS), lambda c: (0, 0)),
            pl.BlockSpec((peers, ROWS, F), lambda c: (0, c, 0)),
        ],
        out_specs=[pl.BlockSpec((ROWS, 2 * F), lambda c: (c, 0))] * 2,
        compiler_params=params,
        cost_estimate=cost(1 << 26, 2 << 20),
    )(held, grads)
    far_sum = lax.ppermute(far_sum, "region", [(r, r + 1) for r in range(regions - 1)])
    inverse = pl.pallas_call(
        fetch_kernel,
        out_shape=shape(inverse.shape),
        in_specs=[pl.BlockSpec(memory_space=pl.ANY)] * 2,
        out_specs=whole(1)[0],
        scratch_shapes=[pltpu.SemaphoreType.DMA],
        compiler_params=pltpu.CompilerParams(vmem_limit_bytes=VMEM_BYTES // 2),
        cost_estimate=cost(0, 4 << 20),
    )(inverse, near_sum)
    adjoint = pl.pallas_call(
        inverse_kernel,
        out_shape=shape((3 * ROWS, ticks)),
        in_specs=whole(3),
        out_specs=whole(1)[0],
        compiler_params=pltpu.CompilerParams(vmem_limit_bytes=VMEM_BYTES // 2),
        cost_estimate=cost(2 * 3 * ROWS * ticks * 2 * F, 3 << 20),
    )(near_sum, far_sum, inverse)
    adjoint = adjoint.reshape(3, ROWS, ticks).transpose(1, 0, 2)
    return (adjoint, misfit)


def solution(mesh):
    both = ("region", "dev")
    placed = (P(both, None, None),) * 2 + (P(both, None),) * 2 + (P(both),) * 4
    return jax.shard_map(
        functools.partial(on_device, mesh.shape["region"]),
        mesh=mesh,
        in_specs=placed,
        out_specs=(P(both, None, None), P(both)),
        check_vma=False,
    )
```

```python
import functools
import math

import jax
import jax.numpy as jnp
import ml_dtypes
import numpy as np
from jax import lax
from jax.experimental import pallas as pl
from jax.experimental.pallas import tpu as pltpu
from jax.sharding import PartitionSpec as P

F = 512
FLOW = 64
LAGS = 512
ZS = 8
YS = 4
CAP = 4
ROWS = 16
Q = 6
RADIX = 4
EARLY, LATE = (0, 1, 2, 3), (4, 5, 6, 7)
VMEM_BYTES = 40 * 1024 * 1024
BF = jnp.bfloat16
F32 = jnp.float32


def tables(ticks):
    rate = FLOW + np.arange(F, dtype=np.int64).reshape(-1, RADIX).T.reshape(-1)
    quarter = ticks // RADIX
    turn = (np.arange(quarter, dtype=np.int64)[:, None] * rate[None, :]) % ticks
    angle = (turn.astype(np.float32) * np.float32(2.0 * math.pi / ticks)).astype(np.float64)
    forward = np.stack([np.cos(angle), -np.sin(angle)], 1).astype(np.float32)
    forward = (forward / np.float32(math.sqrt(ticks))).astype(ml_dtypes.bfloat16)
    forward = forward.reshape(quarter, 2, RADIX, F // RADIX).transpose(2, 0, 1, 3)
    forward = forward.reshape(RADIX, quarter, 2 * F // RADIX)
    shifts = np.arange(LAGS, dtype=np.int64) - LAGS // 2
    turn = (rate[:, None] * shifts[None, :]) % ticks
    angle = (turn.astype(np.float32) * np.float32(2.0 * math.pi / ticks)).astype(np.float64)
    lag = np.concatenate([np.cos(angle), -np.sin(angle)], 0).astype(np.float32)
    lag = (lag / np.float32(math.sqrt(F))).astype(ml_dtypes.bfloat16)
    return forward, np.ascontiguousarray(forward.transpose(0, 2, 1)), lag


def z_pairs(step):
    return [(z * YS + y, (z + step) % ZS * YS + y) for z in range(ZS) for y in range(YS)]


def y_pairs(step, regions, shift):
    devs = ZS * YS
    return [
        (r * devs + z * YS + y, (r + shift) * devs + z * YS + (y + step) % YS)
        for r in range(max(0, -shift), min(regions, regions - shift))
        for z in range(ZS)
        for y in range(YS)
    ]


def iota(shape, axis):
    return lax.broadcasted_iota(jnp.int32, shape, axis)


def dot(a, b):
    return jnp.dot(a, b, preferred_element_type=F32)


def forward_kernel(synthetic_ref, observed_ref, far_table_ref, out_ref, held, table_ref, done):
    quarter = synthetic_ref.shape[2] // RADIX
    group = F // RADIX
    copies = [
        pltpu.make_async_copy(ref, held.at[n], done.at[n])
        for n, ref in enumerate((synthetic_ref, observed_ref))
    ]
    copies += [
        pltpu.make_async_copy(far_table_ref.at[c], table_ref.at[c], done.at[2 + c])
        for c in range(RADIX)
    ]
    for copy in copies[:4]:
        copy.start()
    copies[0].wait()
    copies[1].wait()
    traces = jnp.concatenate([held[n, c] for n in range(2) for c in range(3)], 0)
    for c in range(RADIX):
        copies[2 + c].wait()
        if c + 2 < RADIX:
            copies[4 + c].start()
        sums = [dot(traces[:, j * quarter : (j + 1) * quarter], table_ref[c]) for j in range(RADIX)]
        (r0, i0), (r1, i1), (r2, i2), (r3, i3) = [(p[:, :group], p[:, group:]) for p in sums]
        if c == 0:
            real, imag = (r0 + r1) + (r2 + r3), (i0 + i1) + (i2 + i3)
        elif c == 1:
            real, imag = (r0 - r2) + (i1 - i3), (i0 - i2) - (r1 - r3)
        elif c == 2:
            real, imag = (r0 - r1) + (r2 - r3), (i0 - i1) + (i2 - i3)
        else:
            real, imag = (r0 - r2) - (i1 - i3), (i0 - i2) + (r1 - r3)
        at = c * group
        out_ref[:Q, :, at : at + group] = real.astype(BF).reshape(Q, ROWS, group)
        out_ref[:Q, :, F + at : F + at + group] = imag.astype(BF).reshape(Q, ROWS, group)


def index_kernel(near_ref, far_ref, _, out_ref):
    cap, peers = near_ref.shape
    both = jnp.concatenate([near_ref[...], far_ref[...]], 0).astype(F32)
    both = jnp.concatenate([both, jnp.zeros((2 * cap, 4 * peers - peers), F32)], 1)
    out_ref[Q, :, : 4 * peers] = jnp.concatenate([both, jnp.zeros_like(both)], 0).astype(BF)


def fetch_kernel(source_ref, _, out_ref, done):
    copy = pltpu.make_async_copy(source_ref, out_ref, done)
    copy.start()
    copy.wait()


def inverse_kernel(near_ref, far_ref, table_ref, out_ref):
    rows = out_ref.shape[0]
    quarter = out_ref.shape[1] // RADIX
    group = F // RADIX
    total = (near_ref[...] + far_ref[...].astype(F32)).astype(BF)
    real = [total[:, c * group : (c + 1) * group] for c in range(RADIX)]
    imag = [total[:, F + c * group : F + (c + 1) * group] for c in range(RADIX)]
    plain = [jnp.concatenate([real[c], imag[c]], 1) for c in range(RADIX)]
    turned = [jnp.concatenate([-imag[c], real[c]], 1) for c in range(RADIX)]
    p0, p2 = dot(plain[0], table_ref[0]), dot(plain[2], table_ref[2])
    one = dot(jnp.concatenate([plain[1], turned[1]], 0), table_ref[1])
    three = dot(jnp.concatenate([plain[3], turned[3]], 0), table_ref[3])
    p1, q1, p3, q3 = one[:rows], one[rows:], three[:rows], three[rows:]
    out_ref[:, :quarter] = ((p0 + p2) + (p1 + p3)).astype(BF)
    out_ref[:, quarter : 2 * quarter] = ((p0 - p2) + (q1 - q3)).astype(BF)
    out_ref[:, 2 * quarter : 3 * quarter] = ((p0 + p2) - (p1 + p3)).astype(BF)
    out_ref[:, 3 * quarter :] = ((p0 - p2) - (q1 - q3)).astype(BF)


def position():
    here = lax.axis_index("dev")
    return here // YS, here % YS


def select_kernel(jobs, places, *refs):
    blocks, outs = dict(zip(places, refs)), refs[len(places) :]
    z, y = position()
    for n, (side, ring) in enumerate(jobs):
        out, size = outs[n * YS : (n + 1) * YS], len(ring)
        count, wide = size * CAP, size * ROWS
        row = iota((YS * count, 1), 0)
        cap, block, step = row % CAP, row // CAP % size, row // count
        expand = (iota((YS * count, wide), 1) == block * ROWS + side * CAP + cap).astype(BF)
        index = jnp.concatenate([blocks[p][Q, :, : 4 * ZS * YS] for p in ring], 0)
        spread = dot(expand, index)
        lane = z * YS + (y + step) % YS
        value = jnp.sum(jnp.where(iota(spread.shape, 1) == lane, spread, 0.0), 1, keepdims=True)
        pick = iota((YS * count, wide), 1) == block * ROWS + value.astype(jnp.int32)
        pick = pick.astype(BF)
        for q in range(Q):
            got = dot(pick, jnp.concatenate([blocks[p][q] for p in ring], 0)).astype(BF)
            for k in range(YS):
                out[k][q // 3, q % 3] = got[k * count : (k + 1) * count]


def ring_place(offset):
    offset = offset % ZS
    return jnp.where(offset == 0, 0, jnp.where(offset <= ZS // 2, 2 * offset - 1, 2 * (ZS - offset)))


def pair_kernel(slots_ref, lag_ref, *refs):
    pieces, (misfit_ref, out_ref) = refs[:-2], refs[-2:]
    pairs = slots_ref.shape[1]
    peers = ZS * YS
    near = peers * CAP
    z, y = position()
    lag = lag_ref[...]
    slots = slots_ref[:2]
    side, member, cap = slots // near, slots // CAP % peers, slots % CAP
    step = (y - member % YS + YS) % YS
    held = ((side * YS + step) * ZS + ring_place(z - member // YS + ZS)) * CAP + cap
    back = (member * 2 + side) * CAP + cap
    first_back = (iota((2 * near, pairs), 0) == back[:1]).astype(BF)
    second_back = (iota((2 * near, pairs), 0) == back[1:]).astype(BF)
    column = jnp.concatenate([held, slots_ref[2:4], held, held], 0).astype(F32).T.astype(jnp.int32)
    first = (iota((pairs, near), 1) == column[:, 0:1]).astype(BF)
    second = (iota((pairs, 2 * near), 1) == column[:, 1:2]).astype(BF)

    at = iota((pairs, LAGS), 1)
    start = column[:, 2:3]
    inside = (at >= start) & (at < start + column[:, 3:4])
    kept, reals, imags = [], [], []
    for c in range(3):

        def both(kind):
            spectra = jnp.concatenate([piece[kind, c] for piece in pieces], 0)
            a = dot(first, spectra[:near])
            b = dot(second, spectra)
            return a[:, :F], a[:, F:], b[:, :F], b[:, F:]

        ar, ai, br, bi = both(0)
        cr, ci, dr, di = both(1)
        reals.append(((ar * br + ai * bi) - (cr * dr + ci * di)).astype(BF))
        imags.append(((ai * br - ar * bi) - (ci * dr - cr * di)).astype(BF))
        kept.append([v.astype(BF) for v in (ar, ai, br, bi)])
    shifted = dot(jnp.concatenate(reals, 0), lag[:F]) + dot(jnp.concatenate(imags, 0), lag[F:])
    residuals = [jnp.where(inside, shifted[c * pairs : (c + 1) * pairs], 0.0) for c in range(3)]
    misfit = sum(jnp.sum(r * r, axis=1, keepdims=True) for r in residuals)
    misfit_ref[...] = misfit * (1.0 / (2.0 * LAGS))
    rounded = jnp.concatenate([r.astype(BF) for r in residuals], 0)
    slope = lax.dot_general(rounded, lag, (((1,), (1,)), ((), ())), preferred_element_type=F32)
    for c in range(3):
        ar, ai, br, bi = [v.astype(F32) for v in kept[c]]
        gr, gi = slope[c * pairs : (c + 1) * pairs, :F], slope[c * pairs : (c + 1) * pairs, F:]
        grad_first = jnp.concatenate([gr * br - gi * bi, gr * bi + gi * br], 1).astype(BF)
        grad_second = jnp.concatenate([gr * ar + gi * ai, gr * ai - gi * ar], 1).astype(BF)
        total = dot(first_back, grad_first) + dot(second_back, grad_second)
        total = total.reshape(peers, 2 * CAP, 2 * F)
        total = jnp.concatenate([total[..., :F], total[..., F:]], 1).astype(BF)
        out_ref[:, c * ROWS : (c + 1) * ROWS] = total


def collect_kernel(held_ref, grad_ref, near_ref, far_ref):
    rows = held_ref.shape[1]
    pick = (iota((4 * ROWS, rows), 0) == held_ref[...]).astype(BF)
    total = dot(pick, grad_ref[...].reshape(rows, F))
    near_ref[...] = jnp.concatenate([total[:ROWS], total[2 * ROWS : 3 * ROWS]], 1)
    far_ref[...] = jnp.concatenate([total[ROWS : 2 * ROWS], total[3 * ROWS :]], 1).astype(BF)


def whole(count):
    return [pl.BlockSpec(memory_space=pltpu.VMEM)] * count


def shape(dims, kind=BF):
    return jax.ShapeDtypeStruct(dims, kind)


def cost(flops, size):
    return pl.CostEstimate(flops=flops, bytes_accessed=size, transcendentals=0)


def on_device(
    regions,
    synthetic,
    observed,
    nearby_receiver_slots,
    far_rows,
    first_slot,
    second_slot,
    window_start,
    pair_delay_indices,
):
    ticks = synthetic.shape[2]
    pairs = first_slot.shape[0]
    forward, inverse, lag = [jnp.asarray(table) for table in tables(ticks)]
    params = pltpu.CompilerParams(vmem_limit_bytes=VMEM_BYTES)
    peers = ZS * YS

    def z_move(value, step):
        return lax.ppermute(value, "dev", z_pairs(step))

    def y_move(value, step, shift):
        return lax.ppermute(value, ("region", "dev"), y_pairs(step, regions, shift))

    far_index = lax.ppermute(far_rows.T, "region", [(r, r + 1) for r in range(regions - 1)])
    sources = [synthetic.transpose(1, 0, 2), observed.transpose(1, 0, 2)]
    own = pl.pallas_call(
        forward_kernel,
        out_shape=shape((Q + 1, ROWS, 2 * F)),
        in_specs=[pl.BlockSpec(memory_space=pl.ANY)] * 3,
        out_specs=whole(1)[0],
        scratch_shapes=[
            pltpu.VMEM((2, 3, ROWS, ticks), BF),
            pltpu.VMEM(forward.shape, BF),
            pltpu.SemaphoreType.DMA((2 + RADIX,)),
        ],
        compiler_params=pltpu.CompilerParams(vmem_limit_bytes=63_225_856),
        cost_estimate=cost(2 * Q * ROWS * ticks * 2 * F, 3 << 20),
    )(*sources, forward)
    own = pl.pallas_call(
        index_kernel,
        out_shape=shape(own.shape),
        in_specs=whole(3),
        out_specs=whole(1)[0],
        input_output_aliases={2: 0},
        compiler_params=pltpu.CompilerParams(vmem_limit_bytes=VMEM_BYTES // 2),
        cost_estimate=cost(1 << 20, 1 << 16),
    )(nearby_receiver_slots.T, far_index, own)

    def select(jobs, blocks):
        sizes = [len(ring) * CAP for _, ring in jobs for _ in range(YS)]
        return pl.pallas_call(
            functools.partial(select_kernel, jobs, tuple(blocks)),
            out_shape=[shape((2, 3, size, 2 * F)) for size in sizes],
            in_specs=whole(len(blocks)),
            out_specs=whole(len(sizes)),
            compiler_params=params,
            cost_estimate=cost(1 << 29, 5 << 20),
        )(*blocks.values())

    up, down = z_move(own, 1), z_move(own, -1)
    up2, down2 = z_move(up, 1), z_move(down, -1)
    up3, down3 = z_move(up2, 1), z_move(down2, -1)
    early = select([(0, EARLY)], dict(zip(EARLY, [own, up, down, up2])))
    early = [early[0]] + [y_move(early[k], k, 0) for k in range(1, YS)]
    split = Q // 2
    half_up, half_down = up3[:split], down3[split:]
    half_up, early[0] = lax.optimization_barrier((half_up, early[0]))
    last = jnp.concatenate([z_move(half_up, 1), z_move(half_down, -1)], 0)
    blocks = dict(enumerate([own, up, down, up2, down2, up3, down3, last]))
    late = select([(0, LATE), (1, EARLY + LATE)], blocks)
    far = [y_move(piece, k, -1) for k, piece in enumerate(late[YS:])]
    late = [late[0]] + [y_move(late[k], k, 0) for k in range(1, YS)]
    pieces = [piece for pair in zip(early, late) for piece in pair] + far
    slots = jnp.stack([first_slot, second_slot, window_start, pair_delay_indices])
    misfit, grads = pl.pallas_call(
        pair_kernel,
        out_shape=[shape((pairs, 1), F32), shape((peers, 3 * ROWS, F))],
        in_specs=whole(2 + len(pieces)),
        out_specs=whole(2),
        compiler_params=params,
        cost_estimate=cost(9 << 30, 9 << 20),
    )(slots, lag, *pieces)
    grads = lax.all_to_all(grads, "dev", split_axis=0, concat_axis=0, tiled=True)
    grads, misfit = lax.optimization_barrier((grads, misfit.reshape(pairs)))
    held = jnp.concatenate([nearby_receiver_slots, far_rows + ROWS], 1)
    held = jnp.concatenate([held, held + 2 * ROWS], 1).reshape(1, peers * ROWS)
    near_sum, far_sum = pl.pallas_call(
        collect_kernel,
        grid=(3,),
        out_shape=[shape((3 * ROWS, 2 * F), F32), shape((3 * ROWS, 2 * F))],
        in_specs=[
            pl.BlockSpec((1, peers * ROWS), lambda c: (0, 0)),
            pl.BlockSpec((peers, ROWS, F), lambda c: (0, c, 0)),
        ],
        out_specs=[pl.BlockSpec((ROWS, 2 * F), lambda c: (c, 0))] * 2,
        compiler_params=params,
        cost_estimate=cost(1 << 26, 2 << 20),
    )(held, grads)
    far_sum = lax.ppermute(far_sum, "region", [(r, r + 1) for r in range(regions - 1)])
    inverse = pl.pallas_call(
        fetch_kernel,
        out_shape=shape(inverse.shape),
        in_specs=[pl.BlockSpec(memory_space=pl.ANY)] * 2,
        out_specs=whole(1)[0],
        scratch_shapes=[pltpu.SemaphoreType.DMA],
        compiler_params=pltpu.CompilerParams(vmem_limit_bytes=VMEM_BYTES // 2),
        cost_estimate=cost(0, 4 << 20),
    )(inverse, near_sum)
    adjoint = pl.pallas_call(
        inverse_kernel,
        out_shape=shape((3 * ROWS, ticks)),
        in_specs=whole(3),
        out_specs=whole(1)[0],
        compiler_params=pltpu.CompilerParams(vmem_limit_bytes=VMEM_BYTES // 2),
        cost_estimate=cost(2 * 3 * ROWS * ticks * 2 * F, 3 << 20),
    )(near_sum, far_sum, inverse)
    adjoint = adjoint.reshape(3, ROWS, ticks).transpose(1, 0, 2)
    return (adjoint, misfit)


def solution(mesh):
    both = ("region", "dev")
    placed = (P(both, None, None),) * 2 + (P(both, None),) * 2 + (P(both),) * 4
    return jax.shard_map(
        functools.partial(on_device, mesh.shape["region"]),
        mesh=mesh,
        in_specs=placed,
        out_specs=(P(both, None, None), P(both)),
        check_vma=False,
    )
```

```python
import functools
import math

import jax
import jax.numpy as jnp
import ml_dtypes
import numpy as np
from jax import lax
from jax.experimental import pallas as pl
from jax.experimental.pallas import tpu as pltpu
from jax.sharding import PartitionSpec as P

F = 512
FLOW = 64
LAGS = 512
ZS = 8
YS = 4
CAP = 4
ROWS = 16
Q = 6
RADIX = 4
EARLY, LATE = (0, 1, 2, 3), (4, 5, 6, 7)
VMEM_BYTES = 40 * 1024 * 1024
BF = jnp.bfloat16
F32 = jnp.float32


def tables(ticks):
    rate = FLOW + np.arange(F, dtype=np.int64).reshape(-1, RADIX).T.reshape(-1)
    quarter = ticks // RADIX
    turn = (np.arange(quarter, dtype=np.int64)[:, None] * rate[None, :]) % ticks
    angle = (turn.astype(np.float32) * np.float32(2.0 * math.pi / ticks)).astype(np.float64)
    forward = np.stack([np.cos(angle), -np.sin(angle)], 1).astype(np.float32)
    forward = (forward / np.float32(math.sqrt(ticks))).astype(ml_dtypes.bfloat16)
    forward = forward.reshape(quarter, 2, RADIX, F // RADIX).transpose(2, 0, 1, 3)
    forward = forward.reshape(RADIX, quarter, 2 * F // RADIX)
    shifts = np.arange(LAGS, dtype=np.int64) - LAGS // 2
    turn = (rate[:, None] * shifts[None, :]) % ticks
    angle = (turn.astype(np.float32) * np.float32(2.0 * math.pi / ticks)).astype(np.float64)
    lag = np.concatenate([np.cos(angle), -np.sin(angle)], 0).astype(np.float32)
    lag = (lag / np.float32(math.sqrt(F))).astype(ml_dtypes.bfloat16)
    return forward, np.ascontiguousarray(forward.transpose(0, 2, 1)), lag


def z_pairs(step):
    return [(z * YS + y, (z + step) % ZS * YS + y) for z in range(ZS) for y in range(YS)]


def y_pairs(step, regions, shift):
    devs = ZS * YS
    return [
        (r * devs + z * YS + y, (r + shift) * devs + z * YS + (y + step) % YS)
        for r in range(max(0, -shift), min(regions, regions - shift))
        for z in range(ZS)
        for y in range(YS)
    ]


def iota(shape, axis):
    return lax.broadcasted_iota(jnp.int32, shape, axis)


def dot(a, b):
    return jnp.dot(a, b, preferred_element_type=F32)


def forward_kernel(synthetic_ref, observed_ref, far_table_ref, out_ref, held, table_ref, done):
    quarter = synthetic_ref.shape[2] // RADIX
    group = F // RADIX
    copies = [
        pltpu.make_async_copy(ref, held.at[n], done.at[n])
        for n, ref in enumerate((synthetic_ref, observed_ref))
    ]
    copies += [
        pltpu.make_async_copy(far_table_ref.at[c], table_ref.at[c], done.at[2 + c])
        for c in range(RADIX)
    ]
    for copy in copies[:4]:
        copy.start()
    copies[0].wait()
    copies[1].wait()
    traces = jnp.concatenate([held[n, c] for n in range(2) for c in range(3)], 0)
    for c in range(RADIX):
        copies[2 + c].wait()
        if c + 2 < RADIX:
            copies[4 + c].start()
        sums = [dot(traces[:, j * quarter : (j + 1) * quarter], table_ref[c]) for j in range(RADIX)]
        (r0, i0), (r1, i1), (r2, i2), (r3, i3) = [(p[:, :group], p[:, group:]) for p in sums]
        if c == 0:
            real, imag = (r0 + r1) + (r2 + r3), (i0 + i1) + (i2 + i3)
        elif c == 1:
            real, imag = (r0 - r2) + (i1 - i3), (i0 - i2) - (r1 - r3)
        elif c == 2:
            real, imag = (r0 - r1) + (r2 - r3), (i0 - i1) + (i2 - i3)
        else:
            real, imag = (r0 - r2) - (i1 - i3), (i0 - i2) + (r1 - r3)
        at = c * group
        out_ref[:Q, :, at : at + group] = real.astype(BF).reshape(Q, ROWS, group)
        out_ref[:Q, :, F + at : F + at + group] = imag.astype(BF).reshape(Q, ROWS, group)


def index_kernel(near_ref, far_ref, _, out_ref):
    cap, peers = near_ref.shape
    both = jnp.concatenate([near_ref[...], far_ref[...]], 0).astype(F32)
    both = jnp.concatenate([both, jnp.zeros((2 * cap, 4 * peers - peers), F32)], 1)
    out_ref[Q, :, : 4 * peers] = jnp.concatenate([both, jnp.zeros_like(both)], 0).astype(BF)


def fetch_kernel(source_ref, _, out_ref, done):
    copy = pltpu.make_async_copy(source_ref, out_ref, done)
    copy.start()
    copy.wait()


def inverse_kernel(near_ref, far_ref, table_ref, out_ref):
    rows = out_ref.shape[0]
    quarter = out_ref.shape[1] // RADIX
    group = F // RADIX
    total = (near_ref[...] + far_ref[...].astype(F32)).astype(BF)
    real = [total[:, c * group : (c + 1) * group] for c in range(RADIX)]
    imag = [total[:, F + c * group : F + (c + 1) * group] for c in range(RADIX)]
    plain = [jnp.concatenate([real[c], imag[c]], 1) for c in range(RADIX)]
    turned = [jnp.concatenate([-imag[c], real[c]], 1) for c in range(RADIX)]
    p0, p2 = dot(plain[0], table_ref[0]), dot(plain[2], table_ref[2])
    one = dot(jnp.concatenate([plain[1], turned[1]], 0), table_ref[1])
    three = dot(jnp.concatenate([plain[3], turned[3]], 0), table_ref[3])
    p1, q1, p3, q3 = one[:rows], one[rows:], three[:rows], three[rows:]
    out_ref[:, :quarter] = ((p0 + p2) + (p1 + p3)).astype(BF)
    out_ref[:, quarter : 2 * quarter] = ((p0 - p2) + (q1 - q3)).astype(BF)
    out_ref[:, 2 * quarter : 3 * quarter] = ((p0 + p2) - (p1 + p3)).astype(BF)
    out_ref[:, 3 * quarter :] = ((p0 - p2) - (q1 - q3)).astype(BF)


def position():
    here = lax.axis_index("dev")
    return here // YS, here % YS


def select_kernel(jobs, places, *refs):
    blocks, outs = dict(zip(places, refs)), refs[len(places) :]
    z, y = position()
    for n, (side, ring) in enumerate(jobs):
        out, size = outs[n * YS : (n + 1) * YS], len(ring)
        count, wide = size * CAP, size * ROWS
        row = iota((YS * count, 1), 0)
        cap, block, step = row % CAP, row // CAP % size, row // count
        expand = (iota((YS * count, wide), 1) == block * ROWS + side * CAP + cap).astype(BF)
        index = jnp.concatenate([blocks[p][Q, :, : 4 * ZS * YS] for p in ring], 0)
        spread = dot(expand, index)
        lane = z * YS + (y + step) % YS
        value = jnp.sum(jnp.where(iota(spread.shape, 1) == lane, spread, 0.0), 1, keepdims=True)
        pick = iota((YS * count, wide), 1) == block * ROWS + value.astype(jnp.int32)
        pick = pick.astype(BF)
        for q in range(Q):
            got = dot(pick, jnp.concatenate([blocks[p][q] for p in ring], 0)).astype(BF)
            for k in range(YS):
                out[k][q // 3, q % 3] = got[k * count : (k + 1) * count]


def ring_place(offset):
    offset = offset % ZS
    return jnp.where(offset == 0, 0, jnp.where(offset <= ZS // 2, 2 * offset - 1, 2 * (ZS - offset)))


def pair_kernel(slots_ref, lag_ref, *refs):
    pieces, (misfit_ref, out_ref) = refs[:-2], refs[-2:]
    pairs = slots_ref.shape[1]
    peers = ZS * YS
    near = peers * CAP
    z, y = position()
    lag = lag_ref[...]
    slots = slots_ref[:2]
    side, member, cap = slots // near, slots // CAP % peers, slots % CAP
    step = (y - member % YS + YS) % YS
    held = ((side * YS + step) * ZS + ring_place(z - member // YS + ZS)) * CAP + cap
    back = (member * 2 + side) * CAP + cap
    first_back = (iota((2 * near, pairs), 0) == back[:1]).astype(BF)
    second_back = (iota((2 * near, pairs), 0) == back[1:]).astype(BF)
    column = jnp.concatenate([held, slots_ref[2:4], held, held], 0).astype(F32).T.astype(jnp.int32)
    first = (iota((pairs, near), 1) == column[:, 0:1]).astype(BF)
    second = (iota((pairs, 2 * near), 1) == column[:, 1:2]).astype(BF)

    at = iota((pairs, LAGS), 1)
    start = column[:, 2:3]
    inside = (at >= start) & (at < start + column[:, 3:4])
    kept, reals, imags = [], [], []
    for c in range(3):

        def both(kind):
            spectra = jnp.concatenate([piece[kind, c] for piece in pieces], 0)
            a = dot(first, spectra[:near])
            b = dot(second, spectra)
            return a[:, :F], a[:, F:], b[:, :F], b[:, F:]

        ar, ai, br, bi = both(0)
        cr, ci, dr, di = both(1)
        reals.append(((ar * br + ai * bi) - (cr * dr + ci * di)).astype(BF))
        imags.append(((ai * br - ar * bi) - (ci * dr - cr * di)).astype(BF))
        kept.append([v.astype(BF) for v in (ar, ai, br, bi)])
    shifted = dot(jnp.concatenate(reals, 0), lag[:F]) + dot(jnp.concatenate(imags, 0), lag[F:])
    residuals = [jnp.where(inside, shifted[c * pairs : (c + 1) * pairs], 0.0) for c in range(3)]
    misfit = sum(jnp.sum(r * r, axis=1, keepdims=True) for r in residuals)
    misfit_ref[...] = misfit * (1.0 / (2.0 * LAGS))
    rounded = jnp.concatenate([r.astype(BF) for r in residuals], 0)
    slope = lax.dot_general(rounded, lag, (((1,), (1,)), ((), ())), preferred_element_type=F32)
    for c in range(3):
        ar, ai, br, bi = [v.astype(F32) for v in kept[c]]
        gr, gi = slope[c * pairs : (c + 1) * pairs, :F], slope[c * pairs : (c + 1) * pairs, F:]
        grad_first = jnp.concatenate([gr * br - gi * bi, gr * bi + gi * br], 1).astype(BF)
        grad_second = jnp.concatenate([gr * ar + gi * ai, gr * ai - gi * ar], 1).astype(BF)
        total = dot(first_back, grad_first) + dot(second_back, grad_second)
        total = total.reshape(peers, 2 * CAP, 2 * F)
        total = jnp.concatenate([total[..., :F], total[..., F:]], 1).astype(BF)
        out_ref[:, c * ROWS : (c + 1) * ROWS] = total


def collect_kernel(held_ref, grad_ref, near_ref, far_ref):
    rows = held_ref.shape[1]
    pick = (iota((4 * ROWS, rows), 0) == held_ref[...]).astype(BF)
    total = dot(pick, grad_ref[...].reshape(rows, F))
    near_ref[...] = jnp.concatenate([total[:ROWS], total[2 * ROWS : 3 * ROWS]], 1)
    far_ref[...] = jnp.concatenate([total[ROWS : 2 * ROWS], total[3 * ROWS :]], 1).astype(BF)


def whole(count):
    return [pl.BlockSpec(memory_space=pltpu.VMEM)] * count


def shape(dims, kind=BF):
    return jax.ShapeDtypeStruct(dims, kind)


def cost(flops, size):
    return pl.CostEstimate(flops=flops, bytes_accessed=size, transcendentals=0)


def on_device(
    regions,
    synthetic,
    observed,
    nearby_receiver_slots,
    far_rows,
    first_slot,
    second_slot,
    window_start,
    pair_delay_indices,
):
    ticks = synthetic.shape[2]
    pairs = first_slot.shape[0]
    forward, inverse, lag = [jnp.asarray(table) for table in tables(ticks)]
    params = pltpu.CompilerParams(vmem_limit_bytes=VMEM_BYTES)
    peers = ZS * YS

    def z_move(value, step):
        return lax.ppermute(value, "dev", z_pairs(step))

    def y_move(value, step, shift):
        return lax.ppermute(value, ("region", "dev"), y_pairs(step, regions, shift))

    far_index = lax.ppermute(far_rows.T, "region", [(r, r + 1) for r in range(regions - 1)])
    sources = [synthetic.transpose(1, 0, 2), observed.transpose(1, 0, 2)]
    own = pl.pallas_call(
        forward_kernel,
        out_shape=shape((Q + 1, ROWS, 2 * F)),
        in_specs=[pl.BlockSpec(memory_space=pl.ANY)] * 3,
        out_specs=whole(1)[0],
        scratch_shapes=[
            pltpu.VMEM((2, 3, ROWS, ticks), BF),
            pltpu.VMEM(forward.shape, BF),
            pltpu.SemaphoreType.DMA((2 + RADIX,)),
        ],
        compiler_params=pltpu.CompilerParams(vmem_limit_bytes=63_225_856),
        cost_estimate=cost(2 * Q * ROWS * ticks * 2 * F, 3 << 20),
    )(*sources, forward)
    own = pl.pallas_call(
        index_kernel,
        out_shape=shape(own.shape),
        in_specs=whole(3),
        out_specs=whole(1)[0],
        input_output_aliases={2: 0},
        compiler_params=pltpu.CompilerParams(vmem_limit_bytes=VMEM_BYTES // 2),
        cost_estimate=cost(1 << 20, 1 << 16),
    )(nearby_receiver_slots.T, far_index, own)

    def select(jobs, blocks):
        sizes = [len(ring) * CAP for _, ring in jobs for _ in range(YS)]
        return pl.pallas_call(
            functools.partial(select_kernel, jobs, tuple(blocks)),
            out_shape=[shape((2, 3, size, 2 * F)) for size in sizes],
            in_specs=whole(len(blocks)),
            out_specs=whole(len(sizes)),
            compiler_params=params,
            cost_estimate=cost(1 << 29, 5 << 20),
        )(*blocks.values())

    up, down = z_move(own, 1), z_move(own, -1)
    up2, down2 = z_move(up, 1), z_move(down, -1)
    up3, down3 = z_move(up2, 1), z_move(down2, -1)
    early = select([(0, EARLY)], dict(zip(EARLY, [own, up, down, up2])))
    early = [early[0]] + [y_move(early[k], k, 0) for k in range(1, YS)]
    split = Q // 2
    half_up, half_down = up3[:split], down3[split:]
    half_up, half_down, early[1], early[3] = lax.optimization_barrier(
        (half_up, half_down, early[1], early[3])
    )
    last = jnp.concatenate([z_move(half_up, 1), z_move(half_down, -1)], 0)
    blocks = dict(enumerate([own, up, down, up2, down2, up3, down3, last]))
    late = select([(0, LATE), (1, EARLY + LATE)], blocks)
    far = list(late[YS:])
    late = [late[0]] + [y_move(late[k], k, 0) for k in range(1, YS)]
    *late, early[2], far[0] = lax.optimization_barrier((*late, early[2], far[0]))
    far = [y_move(piece, k, -1) for k, piece in enumerate(far)]
    pieces = [piece for pair in zip(early, late) for piece in pair] + far
    slots = jnp.stack([first_slot, second_slot, window_start, pair_delay_indices])
    misfit, grads = pl.pallas_call(
        pair_kernel,
        out_shape=[shape((pairs, 1), F32), shape((peers, 3 * ROWS, F))],
        in_specs=whole(2 + len(pieces)),
        out_specs=whole(2),
        compiler_params=params,
        cost_estimate=cost(9 << 30, 9 << 20),
    )(slots, lag, *pieces)
    grads = lax.all_to_all(grads, "dev", split_axis=0, concat_axis=0, tiled=True)
    grads, misfit = lax.optimization_barrier((grads, misfit.reshape(pairs)))
    held = jnp.concatenate([nearby_receiver_slots, far_rows + ROWS], 1)
    held = jnp.concatenate([held, held + 2 * ROWS], 1).reshape(1, peers * ROWS)
    near_sum, far_sum = pl.pallas_call(
        collect_kernel,
        grid=(3,),
        out_shape=[shape((3 * ROWS, 2 * F), F32), shape((3 * ROWS, 2 * F))],
        in_specs=[
            pl.BlockSpec((1, peers * ROWS), lambda c: (0, 0)),
            pl.BlockSpec((peers, ROWS, F), lambda c: (0, c, 0)),
        ],
        out_specs=[pl.BlockSpec((ROWS, 2 * F), lambda c: (c, 0))] * 2,
        compiler_params=params,
        cost_estimate=cost(1 << 26, 2 << 20),
    )(held, grads)
    far_sum = lax.ppermute(far_sum, "region", [(r, r + 1) for r in range(regions - 1)])
    inverse = pl.pallas_call(
        fetch_kernel,
        out_shape=shape(inverse.shape),
        in_specs=[pl.BlockSpec(memory_space=pl.ANY)] * 2,
        out_specs=whole(1)[0],
        scratch_shapes=[pltpu.SemaphoreType.DMA],
        compiler_params=pltpu.CompilerParams(vmem_limit_bytes=VMEM_BYTES // 2),
        cost_estimate=cost(0, 4 << 20),
    )(inverse, near_sum)
    adjoint = pl.pallas_call(
        inverse_kernel,
        out_shape=shape((3 * ROWS, ticks)),
        in_specs=whole(3),
        out_specs=whole(1)[0],
        compiler_params=pltpu.CompilerParams(vmem_limit_bytes=VMEM_BYTES // 2),
        cost_estimate=cost(2 * 3 * ROWS * ticks * 2 * F, 3 << 20),
    )(near_sum, far_sum, inverse)
    adjoint = adjoint.reshape(3, ROWS, ticks).transpose(1, 0, 2)
    return (adjoint, misfit)


def solution(mesh):
    both = ("region", "dev")
    placed = (P(both, None, None),) * 2 + (P(both, None),) * 2 + (P(both),) * 4
    return jax.shard_map(
        functools.partial(on_device, mesh.shape["region"]),
        mesh=mesh,
        in_specs=placed,
        out_specs=(P(both, None, None), P(both)),
        check_vma=False,
    )
```

```python
import functools
import math

import jax
import jax.numpy as jnp
import ml_dtypes
import numpy as np
from jax import lax
from jax.experimental import pallas as pl
from jax.experimental.pallas import tpu as pltpu
from jax.sharding import PartitionSpec as P

F = 512
FLOW = 64
LAGS = 512
ZS = 8
YS = 4
CAP = 4
ROWS = 16
Q = 6
RADIX = 4
EARLY, LATE = (0, 1, 2, 3), (4, 5, 6, 7)
VMEM_BYTES = 40 * 1024 * 1024
BF = jnp.bfloat16
F32 = jnp.float32


def tables(ticks):
    rate = FLOW + np.arange(F, dtype=np.int64).reshape(-1, RADIX).T.reshape(-1)
    quarter = ticks // RADIX
    turn = (np.arange(quarter, dtype=np.int64)[:, None] * rate[None, :]) % ticks
    angle = (turn.astype(np.float32) * np.float32(2.0 * math.pi / ticks)).astype(np.float64)
    forward = np.stack([np.cos(angle), -np.sin(angle)], 1).astype(np.float32)
    forward = (forward / np.float32(math.sqrt(ticks))).astype(ml_dtypes.bfloat16)
    forward = forward.reshape(quarter, 2, RADIX, F // RADIX).transpose(2, 0, 1, 3)
    forward = forward.reshape(RADIX, quarter, 2 * F // RADIX)
    shifts = np.arange(LAGS, dtype=np.int64) - LAGS // 2
    turn = (rate[:, None] * shifts[None, :]) % ticks
    angle = (turn.astype(np.float32) * np.float32(2.0 * math.pi / ticks)).astype(np.float64)
    lag = np.concatenate([np.cos(angle), -np.sin(angle)], 0).astype(np.float32)
    lag = (lag / np.float32(math.sqrt(F))).astype(ml_dtypes.bfloat16)
    return forward, np.ascontiguousarray(forward.transpose(0, 2, 1)), lag


def z_pairs(step):
    return [(z * YS + y, (z + step) % ZS * YS + y) for z in range(ZS) for y in range(YS)]


def y_pairs(step, regions, shift):
    devs = ZS * YS
    return [
        (r * devs + z * YS + y, (r + shift) * devs + z * YS + (y + step) % YS)
        for r in range(max(0, -shift), min(regions, regions - shift))
        for z in range(ZS)
        for y in range(YS)
    ]


def iota(shape, axis):
    return lax.broadcasted_iota(jnp.int32, shape, axis)


def dot(a, b):
    return jnp.dot(a, b, preferred_element_type=F32)


def forward_kernel(synthetic_ref, observed_ref, far_table_ref, out_ref, held, table_ref, done):
    quarter = synthetic_ref.shape[2] // RADIX
    group = F // RADIX
    copies = [
        pltpu.make_async_copy(ref, held.at[n], done.at[n])
        for n, ref in enumerate((synthetic_ref, observed_ref))
    ]
    copies += [
        pltpu.make_async_copy(far_table_ref.at[c], table_ref.at[c], done.at[2 + c])
        for c in range(RADIX)
    ]
    for copy in copies[:4]:
        copy.start()
    copies[0].wait()
    copies[1].wait()
    traces = jnp.concatenate([held[n, c] for n in range(2) for c in range(3)], 0)
    for c in range(RADIX):
        copies[2 + c].wait()
        if c + 2 < RADIX:
            copies[4 + c].start()
        sums = [dot(traces[:, j * quarter : (j + 1) * quarter], table_ref[c]) for j in range(RADIX)]
        (r0, i0), (r1, i1), (r2, i2), (r3, i3) = [(p[:, :group], p[:, group:]) for p in sums]
        if c == 0:
            real, imag = (r0 + r1) + (r2 + r3), (i0 + i1) + (i2 + i3)
        elif c == 1:
            real, imag = (r0 - r2) + (i1 - i3), (i0 - i2) - (r1 - r3)
        elif c == 2:
            real, imag = (r0 - r1) + (r2 - r3), (i0 - i1) + (i2 - i3)
        else:
            real, imag = (r0 - r2) - (i1 - i3), (i0 - i2) + (r1 - r3)
        at = c * group
        for q in range(Q):
            rows, low = slice(q * ROWS, (q + 1) * ROWS), 2 * F * q + at
            out_ref[:, low : low + group] = real[rows].astype(BF)
            out_ref[:, F + low : F + low + group] = imag[rows].astype(BF)


def index_kernel(near_ref, far_ref, _, out_ref):
    cap, peers = near_ref.shape
    both = jnp.concatenate([near_ref[...], far_ref[...]], 0).astype(F32)
    both = jnp.concatenate([both, jnp.zeros((2 * cap, 4 * peers - peers), F32)], 1)
    out_ref[:, Q * 2 * F :] = jnp.concatenate([both, jnp.zeros_like(both)], 0).astype(BF)


def fetch_kernel(source_ref, _, out_ref, done):
    copy = pltpu.make_async_copy(source_ref, out_ref, done)
    copy.start()
    copy.wait()


def inverse_kernel(near_ref, far_ref, table_ref, out_ref):
    rows = out_ref.shape[0]
    quarter = out_ref.shape[1] // RADIX
    group = F // RADIX
    total = (near_ref[...] + far_ref[...].astype(F32)).astype(BF)
    real = [total[:, c * group : (c + 1) * group] for c in range(RADIX)]
    imag = [total[:, F + c * group : F + (c + 1) * group] for c in range(RADIX)]
    plain = [jnp.concatenate([real[c], imag[c]], 1) for c in range(RADIX)]
    turned = [jnp.concatenate([-imag[c], real[c]], 1) for c in range(RADIX)]
    p0, p2 = dot(plain[0], table_ref[0]), dot(plain[2], table_ref[2])
    one = dot(jnp.concatenate([plain[1], turned[1]], 0), table_ref[1])
    three = dot(jnp.concatenate([plain[3], turned[3]], 0), table_ref[3])
    p1, q1, p3, q3 = one[:rows], one[rows:], three[:rows], three[rows:]
    out_ref[:, :quarter] = ((p0 + p2) + (p1 + p3)).astype(BF)
    out_ref[:, quarter : 2 * quarter] = ((p0 - p2) + (q1 - q3)).astype(BF)
    out_ref[:, 2 * quarter : 3 * quarter] = ((p0 + p2) - (p1 + p3)).astype(BF)
    out_ref[:, 3 * quarter :] = ((p0 - p2) - (q1 - q3)).astype(BF)


def position():
    here = lax.axis_index("dev")
    return here // YS, here % YS


def select_kernel(jobs, places, *refs):
    blocks, outs = dict(zip(places, refs)), refs[len(places) :]
    z, y = position()
    for n, (side, ring) in enumerate(jobs):
        out, size = outs[n * YS : (n + 1) * YS], len(ring)
        count, wide = size * CAP, size * ROWS
        row = iota((YS * count, 1), 0)
        cap, block, step = row % CAP, row // CAP % size, row // count
        expand = (iota((YS * count, wide), 1) == block * ROWS + side * CAP + cap).astype(BF)
        index = jnp.concatenate([blocks[p][:, Q * 2 * F :] for p in ring], 0)
        spread = dot(expand, index)
        lane = z * YS + (y + step) % YS
        value = jnp.sum(jnp.where(iota(spread.shape, 1) == lane, spread, 0.0), 1, keepdims=True)
        pick = iota((YS * count, wide), 1) == block * ROWS + value.astype(jnp.int32)
        pick = pick.astype(BF)
        for q in range(Q):
            got = dot(pick, jnp.concatenate([blocks[p][:, 2 * F * q : 2 * F * (q + 1)] for p in ring], 0)).astype(BF)
            for k in range(YS):
                out[k][q // 3, q % 3] = got[k * count : (k + 1) * count]


def ring_place(offset):
    offset = offset % ZS
    return jnp.where(offset == 0, 0, jnp.where(offset <= ZS // 2, 2 * offset - 1, 2 * (ZS - offset)))


def pair_kernel(slots_ref, lag_ref, *refs):
    pieces, (misfit_ref, out_ref) = refs[:-2], refs[-2:]
    pairs = slots_ref.shape[1]
    peers = ZS * YS
    near = peers * CAP
    z, y = position()
    lag = lag_ref[...]
    slots = slots_ref[:2]
    side, member, cap = slots // near, slots // CAP % peers, slots % CAP
    step = (y - member % YS + YS) % YS
    held = ((side * YS + step) * ZS + ring_place(z - member // YS + ZS)) * CAP + cap
    back = (member * 2 + side) * CAP + cap
    first_back = (iota((2 * near, pairs), 0) == back[:1]).astype(BF)
    second_back = (iota((2 * near, pairs), 0) == back[1:]).astype(BF)
    column = jnp.concatenate([held, slots_ref[2:4], held, held], 0).astype(F32).T.astype(jnp.int32)
    first = (iota((pairs, near), 1) == column[:, 0:1]).astype(BF)
    second = (iota((pairs, 2 * near), 1) == column[:, 1:2]).astype(BF)

    at = iota((pairs, LAGS), 1)
    start = column[:, 2:3]
    inside = (at >= start) & (at < start + column[:, 3:4])
    kept, reals, imags = [], [], []
    for c in range(3):

        def both(kind):
            spectra = jnp.concatenate([piece[kind, c] for piece in pieces], 0)
            a = dot(first, spectra[:near])
            b = dot(second, spectra)
            return a[:, :F], a[:, F:], b[:, :F], b[:, F:]

        ar, ai, br, bi = both(0)
        cr, ci, dr, di = both(1)
        reals.append(((ar * br + ai * bi) - (cr * dr + ci * di)).astype(BF))
        imags.append(((ai * br - ar * bi) - (ci * dr - cr * di)).astype(BF))
        kept.append([v.astype(BF) for v in (ar, ai, br, bi)])
    shifted = dot(jnp.concatenate(reals, 0), lag[:F]) + dot(jnp.concatenate(imags, 0), lag[F:])
    residuals = [jnp.where(inside, shifted[c * pairs : (c + 1) * pairs], 0.0) for c in range(3)]
    misfit = sum(jnp.sum(r * r, axis=1, keepdims=True) for r in residuals)
    misfit_ref[...] = misfit * (1.0 / (2.0 * LAGS))
    rounded = jnp.concatenate([r.astype(BF) for r in residuals], 0)
    slope = lax.dot_general(rounded, lag, (((1,), (1,)), ((), ())), preferred_element_type=F32)
    for c in range(3):
        ar, ai, br, bi = [v.astype(F32) for v in kept[c]]
        gr, gi = slope[c * pairs : (c + 1) * pairs, :F], slope[c * pairs : (c + 1) * pairs, F:]
        grad_first = jnp.concatenate([gr * br - gi * bi, gr * bi + gi * br], 1).astype(BF)
        grad_second = jnp.concatenate([gr * ar + gi * ai, gr * ai - gi * ar], 1).astype(BF)
        total = dot(first_back, grad_first) + dot(second_back, grad_second)
        total = total.reshape(peers, 2 * CAP, 2 * F)
        total = jnp.concatenate([total[..., :F], total[..., F:]], 1).astype(BF)
        out_ref[:, c * ROWS : (c + 1) * ROWS] = total


def collect_kernel(held_ref, grad_ref, near_ref, far_ref):
    rows = held_ref.shape[1]
    pick = (iota((4 * ROWS, rows), 0) == held_ref[...]).astype(BF)
    total = dot(pick, grad_ref[...].reshape(rows, F))
    near_ref[...] = jnp.concatenate([total[:ROWS], total[2 * ROWS : 3 * ROWS]], 1)
    far_ref[...] = jnp.concatenate([total[ROWS : 2 * ROWS], total[3 * ROWS :]], 1).astype(BF)


def whole(count):
    return [pl.BlockSpec(memory_space=pltpu.VMEM)] * count


def shape(dims, kind=BF):
    return jax.ShapeDtypeStruct(dims, kind)


def cost(flops, size):
    return pl.CostEstimate(flops=flops, bytes_accessed=size, transcendentals=0)


def on_device(
    regions,
    synthetic,
    observed,
    nearby_receiver_slots,
    far_rows,
    first_slot,
    second_slot,
    window_start,
    pair_delay_indices,
):
    ticks = synthetic.shape[2]
    pairs = first_slot.shape[0]
    forward, inverse, lag = [jnp.asarray(table) for table in tables(ticks)]
    params = pltpu.CompilerParams(vmem_limit_bytes=VMEM_BYTES)
    peers = ZS * YS

    def z_move(value, step):
        return lax.ppermute(value, "dev", z_pairs(step))

    def y_move(value, step, shift):
        return lax.ppermute(value, ("region", "dev"), y_pairs(step, regions, shift))

    far_index = lax.ppermute(far_rows.T, "region", [(r, r + 1) for r in range(regions - 1)])
    sources = [synthetic.transpose(1, 0, 2), observed.transpose(1, 0, 2)]
    own = pl.pallas_call(
        forward_kernel,
        out_shape=shape((ROWS, Q * 2 * F + 4 * peers)),
        in_specs=[pl.BlockSpec(memory_space=pl.ANY)] * 3,
        out_specs=whole(1)[0],
        scratch_shapes=[
            pltpu.VMEM((2, 3, ROWS, ticks), BF),
            pltpu.VMEM(forward.shape, BF),
            pltpu.SemaphoreType.DMA((2 + RADIX,)),
        ],
        compiler_params=pltpu.CompilerParams(vmem_limit_bytes=63_225_856),
        cost_estimate=cost(2 * Q * ROWS * ticks * 2 * F, 3 << 20),
    )(*sources, forward)
    own = pl.pallas_call(
        index_kernel,
        out_shape=shape(own.shape),
        in_specs=whole(3),
        out_specs=whole(1)[0],
        input_output_aliases={2: 0},
        compiler_params=pltpu.CompilerParams(vmem_limit_bytes=VMEM_BYTES // 2),
        cost_estimate=cost(1 << 20, 1 << 16),
    )(nearby_receiver_slots.T, far_index, own)

    def select(jobs, blocks):
        sizes = [len(ring) * CAP for _, ring in jobs for _ in range(YS)]
        return pl.pallas_call(
            functools.partial(select_kernel, jobs, tuple(blocks)),
            out_shape=[shape((2, 3, size, 2 * F)) for size in sizes],
            in_specs=whole(len(blocks)),
            out_specs=whole(len(sizes)),
            compiler_params=params,
            cost_estimate=cost(1 << 29, 5 << 20),
        )(*blocks.values())

    up, down = z_move(own, 1), z_move(own, -1)
    up2, down2 = z_move(up, 1), z_move(down, -1)
    up3, down3 = z_move(up2, 1), z_move(down2, -1)
    early = select([(0, EARLY)], dict(zip(EARLY, [own, up, down, up2])))
    early = [early[0]] + [y_move(early[k], k, 0) for k in range(1, YS)]
    split = Q // 2 * 2 * F
    half_up, half_down = up3[:, :split], down3[:, split:]
    half_up, half_down, early[1], early[3] = lax.optimization_barrier(
        (half_up, half_down, early[1], early[3])
    )
    last = jnp.concatenate([z_move(half_up, 1), z_move(half_down, -1)], 1)
    blocks = dict(enumerate([own, up, down, up2, down2, up3, down3, last]))
    late = select([(0, LATE), (1, EARLY + LATE)], blocks)
    far = list(late[YS:])
    late = [late[0]] + [y_move(late[k], k, 0) for k in range(1, YS)]
    *late, early[2], far[0] = lax.optimization_barrier((*late, early[2], far[0]))
    far = [y_move(piece, k, -1) for k, piece in enumerate(far)]
    pieces = [piece for pair in zip(early, late) for piece in pair] + far
    slots = jnp.stack([first_slot, second_slot, window_start, pair_delay_indices])
    misfit, grads = pl.pallas_call(
        pair_kernel,
        out_shape=[shape((pairs, 1), F32), shape((peers, 3 * ROWS, F))],
        in_specs=whole(2 + len(pieces)),
        out_specs=whole(2),
        compiler_params=params,
        cost_estimate=cost(9 << 30, 9 << 20),
    )(slots, lag, *pieces)
    grads = lax.all_to_all(grads, "dev", split_axis=0, concat_axis=0, tiled=True)
    grads, misfit = lax.optimization_barrier((grads, misfit.reshape(pairs)))
    held = jnp.concatenate([nearby_receiver_slots, far_rows + ROWS], 1)
    held = jnp.concatenate([held, held + 2 * ROWS], 1).reshape(1, peers * ROWS)
    near_sum, far_sum = pl.pallas_call(
        collect_kernel,
        grid=(3,),
        out_shape=[shape((3 * ROWS, 2 * F), F32), shape((3 * ROWS, 2 * F))],
        in_specs=[
            pl.BlockSpec((1, peers * ROWS), lambda c: (0, 0)),
            pl.BlockSpec((peers, ROWS, F), lambda c: (0, c, 0)),
        ],
        out_specs=[pl.BlockSpec((ROWS, 2 * F), lambda c: (c, 0))] * 2,
        compiler_params=params,
        cost_estimate=cost(1 << 26, 2 << 20),
    )(held, grads)
    far_sum = lax.ppermute(far_sum, "region", [(r, r + 1) for r in range(regions - 1)])
    inverse = pl.pallas_call(
        fetch_kernel,
        out_shape=shape(inverse.shape),
        in_specs=[pl.BlockSpec(memory_space=pl.ANY)] * 2,
        out_specs=whole(1)[0],
        scratch_shapes=[pltpu.SemaphoreType.DMA],
        compiler_params=pltpu.CompilerParams(vmem_limit_bytes=VMEM_BYTES // 2),
        cost_estimate=cost(0, 4 << 20),
    )(inverse, near_sum)
    adjoint = pl.pallas_call(
        inverse_kernel,
        out_shape=shape((3 * ROWS, ticks)),
        in_specs=whole(3),
        out_specs=whole(1)[0],
        compiler_params=pltpu.CompilerParams(vmem_limit_bytes=VMEM_BYTES // 2),
        cost_estimate=cost(2 * 3 * ROWS * ticks * 2 * F, 3 << 20),
    )(near_sum, far_sum, inverse)
    adjoint = adjoint.reshape(3, ROWS, ticks).transpose(1, 0, 2)
    return (adjoint, misfit)


def solution(mesh):
    both = ("region", "dev")
    placed = (P(both, None, None),) * 2 + (P(both, None),) * 2 + (P(both),) * 4
    return jax.shard_map(
        functools.partial(on_device, mesh.shape["region"]),
        mesh=mesh,
        in_specs=placed,
        out_specs=(P(both, None, None), P(both)),
        check_vma=False,
    )
```
